256 devices in a mesh: stack: 16 (over y, z_lo, core), tile: 16 (over z_hi, x).
Axes of the slice: x: 4, y: 4, z: 8 (z_hi: 4, z_lo: 2; z = z_hi * 2 + z_lo), core: 2. Of those that a mesh axis runs over, the one named last changes fastest.
Arguments:
- patches: bfloat16 [128, 4096, 128], P('stack', 'tile'), may hold values from -6 to 6
- candidates: int32 [128, 2, 8, 4096], P('stack', None, None, 'tile'), may hold values from 0 to 4095, as said below
- offsets: int32 [128, 2, 2, 8, 4096], P('stack', None, None, None, 'tile'), may hold values from -64 to 63
- pairs: int32 [128, 2], P('stack'), may hold values 0 or 1
- start: float32 [128, 2, 4096], P('stack', None, 'tile'), may hold values from -3 to 3
Outputs:
- aligned: float32 [128, 2, 4096], P('stack', None, 'tile')
- targets: float32 [128, 2, 2, 4096], P('stack', None, None, 'tile')
The draws below stay inside these ranges and needn't reach their ends.
Inputs may be any that keep to these rules, and one draw needn't show every extreme that they name: Each candidate of a vertex lies at most 2 mesh rows and 2 mesh columns from the vertex, clipped to the mesh; the candidates of one vertex differ except where clipping merges them.
All inputs are finite; a program needn't handle non-finite values. No bound on the sum of `pairs` on one device may be relied on, other than what follows from the above.
Results may differ from the reference program's by a relative error of at most 0.00045.
Values may be sent and summed in bfloat16 or wider, within the bound.
No kernel may reach another device: no remote copies, remote signals or barrier semaphores. Data moves between devices by JAX's collectives and lax.ppermute only.
A program may use at most 64 MiB of HBM per device.

```python
import jax
import jax.numpy as jnp
from jax import lax

TILE_SIDE = 16
GRID_COLS = 4
PATCH = 128
CAND = 8
REACH = 2
ROUNDS = 2
VT = 256
VERTS = 4096
MESH_COLS = 64
MESH_ROWS = 64
SECTIONS = 128
N_TILE = 16


def draw_candidates(key, part):
    key = jax.random.fold_in(key, 11)
    span = 2 * REACH + 1
    raw = jax.random.randint(key, (SECTIONS, 2, span * span, VERTS), 0, 1 << 20)
    keyed = raw * (span * span) + jnp.arange(span * span, dtype=jnp.int32)[None, None, :, None]
    order = jnp.argsort(keyed, axis=2)[:, :, :CAND]
    step_r = order // span - REACH
    step_c = order % span - REACH
    ids = jnp.arange(VERTS, dtype=jnp.int32)
    tile = ids // VT
    inner = ids % VT
    row = tile // GRID_COLS * TILE_SIDE + inner // TILE_SIDE
    col = tile % GRID_COLS * TILE_SIDE + inner % TILE_SIDE
    new_r = jnp.clip(row + step_r, 0, MESH_ROWS - 1)
    new_c = jnp.clip(col + step_c, 0, MESH_COLS - 1)
    new_t = new_r // TILE_SIDE * GRID_COLS + new_c // TILE_SIDE
    return (new_t * VT + new_r % TILE_SIDE * TILE_SIDE + new_c % TILE_SIDE).astype(jnp.int32)


def draw_patches(key, part):
    key = jax.random.fold_in(key, 23)
    values = jax.random.truncated_normal(key, -6.0, 6.0, (SECTIONS, VERTS, PATCH), jnp.float32)
    return values.astype(jnp.bfloat16)


def with_ends(drawn, stream_key, low, high):
    spot = [jax.random.randint(jax.random.fold_in(stream_key, axis), (), 0, length) for axis, length in enumerate(drawn.shape)]
    longest = drawn.shape.index(max(drawn.shape))
    beside = spot[:longest] + [(spot[longest] + 1) % drawn.shape[longest]] + spot[longest + 1:]
    return drawn.at[tuple(spot)].set(low).at[tuple(beside)].set(high)


def steps_of(rng, shape, cuts, smallest, largest):
    loudness = 1.0
    for dim, blocks in cuts:
        draws = jax.random.uniform(jax.random.fold_in(jax.random.fold_in(rng, 6), dim), (blocks,), jnp.float32, smallest / len(cuts), largest / len(cuts))
        loudness = loudness * jnp.repeat(jnp.exp(draws), shape[dim] // blocks).reshape((-1,) + (1,) * (len(shape) - 1 - dim))
    return loudness


def bell_draw(key, extent, spread, limit, pieces=(), held_as=jnp.bfloat16):
    values = spread * jax.random.normal(key, extent, jnp.float32)
    if pieces:
        values = values * steps_of(key, extent, pieces, -0.22, 0.18)
    return jnp.clip(values, -limit, limit).astype(held_as)


def setup_inputs(seed: int = 0) -> dict:
    arg_keys = jax.random.split(jax.random.key(seed), 6)
    patches = draw_patches(jax.random.fold_in(arg_keys[5], 71), 0)
    candidates = draw_candidates(jax.random.fold_in(arg_keys[5], 71), 0)
    offsets = with_ends(jax.random.randint(arg_keys[2], (SECTIONS, 2, 2, CAND, VERTS), -64, 64), jax.random.fold_in(arg_keys[2], 1), -64, 63).astype(jnp.int32)
    pairs = with_ends((jax.random.randint(arg_keys[3], (SECTIONS, 2), 0, 8) < 7).astype(jnp.int32), jax.random.fold_in(arg_keys[3], 1), 0, 1)
    start = bell_draw(arg_keys[4], (SECTIONS, 2, VERTS), 0.5, 3.0, ((0, 16), (2, 16)), jnp.float32)
    return {"patches": patches, "candidates": candidates, "offsets": offsets, "pairs": pairs, "start": start}


pixel_pitch = 128.0
relax_step = 0.1


def place(ids):
    tile = ids // VT
    inner = ids % VT
    row = (tile // GRID_COLS) * TILE_SIDE + inner // TILE_SIDE
    col = (tile % GRID_COLS) * TILE_SIDE + inner % TILE_SIDE
    return row.astype(jnp.float32), col.astype(jnp.float32)


def laplace(u):
    tile_rows = N_TILE // GRID_COLS
    grid = u.reshape(SECTIONS, 2, tile_rows, GRID_COLS, TILE_SIDE, TILE_SIDE)
    grid = grid.transpose(0, 1, 2, 4, 3, 5).reshape(SECTIONS, 2, MESH_ROWS, MESH_COLS)
    flux_r = grid[:, :, 1:, :] - grid[:, :, :-1, :]
    flux_c = grid[:, :, :, 1:] - grid[:, :, :, :-1]
    zero = ((0, 0), (0, 0))
    lap_r = jnp.pad(flux_r, zero + ((0, 1), (0, 0))) - jnp.pad(flux_r, zero + ((1, 0), (0, 0)))
    lap_c = jnp.pad(flux_c, zero + ((0, 0), (0, 1))) - jnp.pad(flux_c, zero + ((0, 0), (1, 0)))
    lap = lap_r + lap_c
    lap = lap.reshape(SECTIONS, 2, tile_rows, TILE_SIDE, GRID_COLS, TILE_SIDE).transpose(0, 1, 2, 4, 3, 5)
    return lap.reshape(SECTIONS, 2, VERTS)


def reference(patches, candidates, offsets, pairs, start):
    ids = jnp.arange(VERTS, dtype=jnp.int32)
    own_r, own_c = place(ids)

    def one(sec):
        mine = lax.dynamic_index_in_dim(patches, sec, 0, keepdims=False).astype(jnp.float32)
        cand_s = lax.dynamic_index_in_dim(candidates, sec, 0, keepdims=False)
        off_s = lax.dynamic_index_in_dim(offsets, sec, 0, keepdims=False).astype(jnp.float32)
        result = []
        for zed in range(2):
            target = jnp.minimum(sec + zed + 1, SECTIONS - 1).astype(jnp.int32)
            valid = sec + zed + 1 < SECTIONS
            other = lax.dynamic_index_in_dim(patches, target, 0, keepdims=False)
            picked = jnp.take(other, cand_s[zed], axis=0).astype(jnp.float32)
            score = jnp.sum(picked * mine[None], axis=-1) * (PATCH ** -0.5)
            weight = jax.nn.softmax(score, axis=0)
            cand_r, cand_c = place(cand_s[zed])
            row = jnp.sum(weight * (cand_r + off_s[zed, 0] / pixel_pitch), axis=0) - own_r
            col = jnp.sum(weight * (cand_c + off_s[zed, 1] / pixel_pitch), axis=0) - own_c
            pair = jnp.stack([row, col])
            result.append(jnp.where(valid, pair, jnp.zeros_like(pair)))
        return jnp.stack(result)

    targets = lax.map(one, jnp.arange(SECTIONS, dtype=jnp.int32))
    sec_ids = jnp.arange(SECTIONS, dtype=jnp.int32)[:, None]
    zeds = jnp.arange(2, dtype=jnp.int32)[None, :]
    coupling = jnp.where(sec_ids + zeds + 1 < SECTIONS, pairs.astype(jnp.float32), jnp.float32(0.0))
    u = start
    for step in range(ROUNDS):
        padded = jnp.concatenate([u, jnp.zeros((2, 2, VERTS), jnp.float32)], axis=0)
        zforce = jnp.zeros_like(u)
        for zed in range(2):
            spring = coupling[:, zed, None, None] * (padded[zed + 1:zed + 1 + SECTIONS] - u - targets[:, zed])
            moved = jnp.concatenate([jnp.zeros((zed + 1, 2, VERTS), jnp.float32), spring[:SECTIONS - zed - 1]], axis=0)
            zforce = zforce + spring - moved
        plane = laplace(u)
        u = u + relax_step * (plane + zforce)
    return u, targets
```

```python
import jax
import jax.numpy as jnp
from jax import lax
from jax.experimental import pallas as pl
from jax.experimental.pallas import tpu as pltpu
from jax.sharding import PartitionSpec as P

SIDE = 16
COLS = 4
PATCH = 128
VT = 256
HALF = 128
SEC = 8
PITCH = 128.0
STEP = 0.1
BF = jnp.bfloat16
F32 = jnp.float32
I32 = jnp.int32

X_ROWS = 8 * 32 + 64
R_ROWS = 8 * 32 + 64 + 32
S_ROWS = 816
CROSS = ((6, 1), (7, 0), (7, 1))


def swapped(block, axis, partner):
    return lax.ppermute(block, axis, [(i, partner(i)) for i in range(lax.axis_size(axis))])


def col_a(i):
    return i ^ 1


def col_b(i):
    return i // COLS * COLS + (COLS - 1 - i % COLS)


def row_a(i):
    return i ^ COLS


def row_b(i):
    return (COLS - 1 - i // COLS) * COLS + i % COLS


def stack_a(i):
    return i ^ 1


def stack_b(i):
    return (((i + 1) ^ 1) - 1) % 16


def tile_place():
    tile = lax.axis_index("tile").astype(I32)
    return tile // COLS, tile % COLS


def iota(shape, dim):
    return lax.broadcasted_iota(I32, shape, dim)


def two_parts(u):
    hi = u.astype(BF)
    return hi, (u - hi.astype(F32)).astype(BF)


def rows_of(start_ref, scr, first=0):
    for s in range(SEC):
        scr[first + 2 * s : first + 2 * s + 2, :] = start_ref[s]


def dot(a, b):
    return lax.dot_general(a, b, (((1,), (0,)), ((), ())), preferred_element_type=F32)


def dot_t(a, b):
    return lax.dot_general(a, b, (((1,), (1,)), ((), ())), preferred_element_type=F32)


def pack_cols(patches, start, xa, xb, scr):
    _, col = tile_place()
    off_a = jnp.where(col % 2 == 0, SIDE - 2, 0)
    j = iota((64, VT), 0)
    v = iota((64, VT), 1)
    off = jnp.where(j < 32, off_a, SIDE - 2 - off_a)
    source = (j % SIDE) * SIDE + off + (j % 32) // SIDE
    pick = (v == source).astype(BF)
    for s in range(SEC):
        strips = dot(pick, patches[s]).astype(BF)
        xa[s * 32 : s * 32 + 32, :] = strips[:32]
        xb[s * 32 : s * 32 + 32, :] = strips[32:]
    rows_of(start, scr)
    hi, lo = two_parts(scr[...])
    for n, part in enumerate((hi[:, :HALF], hi[:, HALF:], lo[:, :HALF], lo[:, HALF:])):
        xa[256 + 16 * n : 272 + 16 * n, :] = part
        xb[256 + 16 * n : 272 + 16 * n, :] = part


def pack_rows(patches, start, xa, xb, ra, rb, scr):
    row, col = tile_place()
    off_a = jnp.where(row % 2 == 0, SIDE - 2, 0)
    off_b = SIDE - 2 - off_a
    for out, off in ((ra, off_a), (rb, off_b)):
        first = pl.multiple_of(off * SIDE, 32)
        for s in range(SEC):
            out[s * 32 : s * 32 + 32, :] = patches[s, pl.ds(first, 32), :]
    both = jnp.concatenate([xa[0:256, :], xb[0:256, :]], axis=0)
    q = iota((128, 512), 0)
    k = iota((128, 512), 1)
    off = jnp.where(q < 64, off_a, off_b)
    side = (q % 8) // 4
    buffer = jnp.where(col % 2 == 0, 1 - side, side)
    source = buffer * 256 + (q % 64) // 8 * 32 + (q % 4) // 2 * SIDE + off + q % 2
    corners = dot((k == source).astype(BF), both).astype(BF)
    ra[256:320, :] = corners[:64]
    rb[256:320, :] = corners[64:]
    rows_of(start, scr)
    hi, lo = two_parts(scr[...])
    even = row % 2 == 0
    for out, second in ((ra, even), (rb, jnp.logical_not(even))):

        @pl.when(second)
        def _():
            out[320:336, :] = hi[:, HALF:]
            out[336:352, :] = lo[:, HALF:]

        @pl.when(jnp.logical_not(second))
        def _():
            out[320:336, :] = hi[:, :HALF]
            out[336:352, :] = lo[:, :HALF]


def local_place(ids, row, col):
    tile = ids >> 8
    lr = (tile >> 2) * SIDE + ((ids >> 4) & 15) - row * SIDE
    lc = (tile & 3) * SIDE + (ids & 15) - col * SIDE
    return lr, lc


def pack_stack(patches, cand, offs, pairs, start, xa, xb, ra, rb, sa, sb, scr):
    row, col = tile_place()
    col_even = col % 2 == 0
    row_even = row % 2 == 0
    stack_even = lax.axis_index("stack") % 2 == 0
    rows_of(start, scr)
    hi, lo = two_parts(scr[...])

    def down(out):
        for s in range(2):
            out[s * 256 : s * 256 + 256, :] = patches[s]
        for even, left, right in ((True, xb, xa), (False, xa, xb)):

            @pl.when(col_even == even)
            def _():
                for s in range(2):
                    out[512 + 64 * s : 544 + 64 * s, :] = left[32 * s : 32 * s + 32, :]
                    out[544 + 64 * s : 576 + 64 * s, :] = right[32 * s : 32 * s + 32, :]

        for even, above, below in ((True, rb, ra), (False, ra, rb)):

            @pl.when(row_even == even)
            def _():
                for s in range(2):
                    out[640 + 64 * s : 672 + 64 * s, :] = above[32 * s : 32 * s + 32, :]
                    out[672 + 64 * s : 704 + 64 * s, :] = below[32 * s : 32 * s + 32, :]
                out[768:784, :] = above[256:272, :]
                out[784:800, :] = below[256:272, :]

        ends(out, 0)

    def up(out):
        for s in range(2):
            out[s * 256 : s * 256 + 256, :] = patches[6 + s]
        for p, (s, z) in enumerate(CROSS):
            lr, lc = local_place(cand[s, z], row, col)
            for n, plane in enumerate((lr, lc, offs[s, z, 0], offs[s, z, 1])):
                at = 512 + 64 * p + 16 * n
                plane = plane.astype(F32)
                out[at : at + 16, :] = jnp.concatenate([plane[:, :HALF], plane[:, HALF:]], axis=0).astype(BF)
        r = iota((16, HALF), 0)
        tied = jnp.zeros((16, HALF), F32)
        for p, (s, z) in enumerate(CROSS):
            tied = jnp.where(r == p, pairs[s, z].astype(F32), tied)
        out[704:720, :] = tied.astype(BF)
        out[720:800, :] = jnp.zeros((80, HALF), BF)
        ends(out, 12)

    def ends(out, first):
        u = scr[first : first + 4, :]
        h, low = two_parts(u)
        h, low = h.astype(F32), low.astype(F32)
        out[800:816, :] = jnp.concatenate(
            [h[:, :HALF], h[:, HALF:], low[:, :HALF], low[:, HALF:]], axis=0
        ).astype(BF)

    @pl.when(stack_even)
    def _():
        up(sa)
        down(sb)

    @pl.when(jnp.logical_not(stack_even))
    def _():
        up(sb)
        down(sa)


def half_targets(h, mine, pieces, corner, lr, lc, off_r, off_c):
    own, left, right, above, below = pieces
    own = own[0:160] if h == 0 else own[96:256]
    centre = [above, own] if h == 0 else [own, below]
    table = jnp.concatenate(centre + [left, right, corner[0]], axis=0)
    scores = dot_t(table, mine)
    first = corner[1]
    i = lr + 2 if h == 0 else lr - 6
    outside_c = (lc < 0) | (lc >= SIDE)
    outside_r = (lr < 0) | (lr >= SIDE)
    low_c = lc & 1
    side = jnp.where(lc >= SIDE, 1, 0)
    slot = i * 2 + (lc >> 3)
    sub = lc & 7
    slot = jnp.where(outside_c, 24 + side * 4 + low_c * 2 + (lr >> 3), slot)
    sub = jnp.where(outside_c, lr & 7, sub)
    corner_hit = outside_c & outside_r
    slot = jnp.where(corner_hit, 32, slot)
    sub = jnp.where(corner_hit, side * 4 + low_c * 2 + (lr & 1), sub)
    score = jnp.zeros((8, HALF), F32)
    for n in range(33):
        at = n * 8 if n < 32 else 256 + first
        got = jnp.take_along_axis(scores[at : at + 8], sub, axis=0)
        score = jnp.where(slot == n, got, score)
    score = score * PATCH ** (-0.5)
    e = jnp.exp(score - jnp.max(score, axis=0, keepdims=True))
    lane = iota((8, HALF), 1)
    step_r = (lr - (lane >> 4) - 8 * h).astype(F32) + off_r * (1.0 / PITCH)
    step_c = (lc - (lane & 15)).astype(F32) + off_c * (1.0 / PITCH)
    total = jnp.sum(e, axis=0, keepdims=True)
    t_r = jnp.sum(e * step_r, axis=0, keepdims=True) / total
    t_c = jnp.sum(e * step_c, axis=0, keepdims=True) / total
    return jnp.concatenate([t_r, t_c], axis=0)


def own_targets(patches, cand, offs, xa, xb, ra, rb, t0, t1, left, right, above, below):
    row, col = tile_place()
    sort_halos(row, col, xa, xb, ra, rb, left, right, above, below)

    def one(s, z, store, corner_first):
        d = s + z + 1

        def strip(ref):
            return ref[pl.ds(pl.multiple_of(d * 32, 32), 32), :]

        pieces = (patches[d], strip(left), strip(right), strip(above), strip(below))
        for h in range(2):
            src = above if h == 0 else below
            at = pl.multiple_of(256 + d // 2 * 16, 16)
            corner = (src[pl.ds(at, 16), :], corner_first)
            lanes = slice(h * HALF, h * HALF + HALF)
            lr, lc = local_place(cand[s, z, :, lanes], row, col)
            got = half_targets(
                h,
                patches[s, lanes, :],
                pieces,
                corner,
                lr,
                lc,
                offs[s, z, 0, :, lanes].astype(F32),
                offs[s, z, 1, :, lanes].astype(F32),
            )
            store[s, :, lanes] = got

    def body(n, carry):
        one(2 * n, 0, t0, 8)
        one(2 * n, 1, t1, 0)
        one(2 * n + 1, 0, t0, 0)
        one(2 * n + 1, 1, t1, 8)
        return carry

    t0[7] = jnp.zeros((2, VT), F32)
    t1[6] = jnp.zeros((2, VT), F32)
    t1[7] = jnp.zeros((2, VT), F32)
    lax.fori_loop(0, 3, body, 0)
    one(6, 0, t0, 8)


def sort_halos(row, col, xa, xb, ra, rb, left, right, above, below):
    for index, first, second, p, q in ((col, left, right, xa, xb), (row, above, below, ra, rb)):

        @pl.when(index % 2 == 0)
        def _():
            first[...] = q[...]
            second[...] = p[...]

        @pl.when(index % 2 == 1)
        def _():
            first[...] = p[...]
            second[...] = q[...]


def laplace(u, left, right, above, below, row, col):
    lane = iota(u.shape, 1)
    b = lane & 15
    up = jnp.where(lane < SIDE, pltpu.roll(above, SIDE, 1), pltpu.roll(u, SIDE, 1))
    up = jnp.where((lane < SIDE) & (row == 0), u, up)
    down = jnp.where(lane >= VT - SIDE, pltpu.roll(below, VT - SIDE, 1), pltpu.roll(u, VT - SIDE, 1))
    down = jnp.where((lane >= VT - SIDE) & (row == COLS - 1), u, down)
    west = jnp.where(b == 0, pltpu.roll(left, VT - SIDE + 1, 1), pltpu.roll(u, 1, 1))
    west = jnp.where((b == 0) & (col == 0), u, west)
    east = jnp.where(b == SIDE - 1, pltpu.roll(right, SIDE - 1, 1), pltpu.roll(u, VT - 1, 1))
    east = jnp.where((b == SIDE - 1) & (col == COLS - 1), u, east)
    return ((down - u) - (u - up)) + ((east - u) - (u - west))


def relaxed(u, tall, t0, t1, c0, c1, plane):
    base = tall[0:20, :]
    s0 = c0[0:20, :] * (tall[2:22, :] - base - t0[0:20, :])
    s1 = c1[0:20, :] * (tall[4:24, :] - base - t1[0:20, :])
    zforce = s0[4:20] - s0[2:18] + s1[4:20] - s1[0:16]
    return u + STEP * (plane + zforce)


def first_round(
    patches, cand, offs, pairs, start, xa, xb, ra, rb, sa, sb, p0, p1,
    targets, u1, t0, t1, c0, c1,
    left, right, above, below, upper, lower, tall,
):
    row, col = tile_place()
    stack = lax.axis_index("stack").astype(I32)
    sort_halos(row, col, xa, xb, ra, rb, left, right, above, below)

    @pl.when(stack % 2 == 0)
    def _():
        upper[...] = sa[...]
        lower[...] = sb[...]

    @pl.when(stack % 2 == 1)
    def _():
        upper[...] = sb[...]
        lower[...] = sa[...]

    def pieces_of(d):
        if d < SEC:
            return (
                patches[d],
                left[32 * d : 32 * d + 32, :],
                right[32 * d : 32 * d + 32, :],
                above[32 * d : 32 * d + 32, :],
                below[32 * d : 32 * d + 32, :],
            ), (above[256 + d // 2 * 16 : 272 + d // 2 * 16, :], below[256 + d // 2 * 16 : 272 + d // 2 * 16, :])
        e = d - SEC
        return (
            upper[256 * e : 256 * e + 256, :],
            upper[512 + 64 * e : 544 + 64 * e, :],
            upper[544 + 64 * e : 576 + 64 * e, :],
            upper[640 + 64 * e : 672 + 64 * e, :],
            upper[672 + 64 * e : 704 + 64 * e, :],
        ), (upper[768:784, :], upper[784:800, :])

    rows_of(p0, t0, 4)
    rows_of(p1, t1, 4)
    t0[0:4, :] = jnp.zeros((4, VT), F32)
    t1[0:4, :] = jnp.zeros((4, VT), F32)
    c0[0:4, :] = jnp.zeros((4, VT), F32)
    c1[0:4, :] = jnp.zeros((4, VT), F32)
    for s in range(SEC):
        for z, c in ((0, c0), (1, c1)):
            c[4 + 2 * s : 6 + 2 * s, :] = jnp.full((2, VT), pairs[s, z], I32).astype(F32)
    last = stack == lax.axis_size("stack") - 1
    tied = jnp.where(stack == 0, 0.0, lower[704:720, :].astype(F32))
    for p, (s, z) in enumerate(CROSS):
        t, c = ((t0, c0), (t1, c1))[z]
        pieces, corners = pieces_of(s + z + 1)
        corner_first = 8 * ((s + z + 1) % 2)
        for h in range(2):
            lanes = slice(h * HALF, h * HALF + HALF)
            lr, lc = local_place(cand[s, z, :, lanes], row, col)
            got = half_targets(
                h, patches[s, lanes, :], pieces, (corners[h], corner_first), lr, lc,
                offs[s, z, 0, :, lanes].astype(F32), offs[s, z, 1, :, lanes].astype(F32),
            )
            t[4 + 2 * s : 6 + 2 * s, lanes] = jnp.where(last, 0.0, got)
        c[4 + 2 * s : 6 + 2 * s, :] = jnp.where(last, 0.0, c[4 + 2 * s : 6 + 2 * s, :])
        d = s + z + 1 - SEC
        pieces, corners = pieces_of(d)
        mine = lower[256 * (s - 6) : 256 * (s - 6) + 256, :]
        planes = [lower[512 + 64 * p + 16 * n : 528 + 64 * p + 16 * n, :].astype(F32) for n in range(4)]
        for h in range(2):
            lanes = slice(h * HALF, h * HALF + HALF)
            lr, lc, off_r, off_c = [plane[8 * h : 8 * h + 8] for plane in planes]
            got = half_targets(
                h, mine[lanes, :], pieces, (corners[h], 8 * (d % 2)),
                lr.astype(I32), lc.astype(I32), off_r, off_c,
            )
            t[2 * (s - 6) : 2 * (s - 6) + 2, lanes] = got
        line = tied[p : p + 1, :]
        c[2 * (s - 6) : 2 * (s - 6) + 2, :] = jnp.broadcast_to(
            jnp.concatenate([line, line], axis=1), (2, VT)
        )
    for s in range(SEC):
        for z, t in ((0, t0), (1, t1)):
            targets[s, z] = t[4 + 2 * s : 6 + 2 * s, :]
    rows_of(start, tall, 4)
    for at, ref in ((0, lower), (20, upper)):
        ends = ref[800:816, :].astype(F32)
        tall[at : at + 4, 0:HALF] = ends[0:4] + ends[8:12]
        tall[at : at + 4, HALF:VT] = ends[4:8] + ends[12:16]
    u = tall[4:20, :]

    def whole(ref):
        part = [ref[256 + 16 * n : 272 + 16 * n, :].astype(F32) for n in range(4)]
        return jnp.concatenate([part[0] + part[2], part[1] + part[3]], axis=1)

    def half(ref):
        part = ref[320:336, :].astype(F32) + ref[336:352, :].astype(F32)
        return jnp.concatenate([part, part], axis=1)

    plane = laplace(u, whole(left), whole(right), half(above), half(below), row, col)
    u1[...] = relaxed(u, tall, t0, t1, c0, c1, plane)


def second_round(u1, xa, xb, ra, rb, sa, sb, t0, t1, c0, c1, out, tall):
    row, col = tile_place()
    stack = lax.axis_index("stack").astype(I32)
    col_even, row_even, stack_even = col % 2 == 0, row % 2 == 0, stack % 2 == 0
    u = u1[...]
    tall[4:20, :] = u
    tall[0:4, :] = jnp.where(stack_even, sb[12:16, :], sa[12:16, :])
    tall[20:24, :] = jnp.where(stack_even, sa[0:4, :], sb[0:4, :])
    plane = laplace(
        u,
        jnp.where(col_even, xb[...], xa[...]),
        jnp.where(col_even, xa[...], xb[...]),
        jnp.where(row_even, rb[...], ra[...]),
        jnp.where(row_even, ra[...], rb[...]),
        row,
        col,
    )
    u = relaxed(u, tall, t0, t1, c0, c1, plane)
    for s in range(SEC):
        out[s] = u[2 * s : 2 * s + 2]


def shape(*dims, dtype=F32):
    return jax.ShapeDtypeStruct(dims, dtype)


def call(body, outs, scratch, name, flops, smem=(), n_in=0, nbytes=1 << 20):
    specs = [
        pl.BlockSpec(memory_space=pltpu.SMEM) if n in smem else pl.BlockSpec(memory_space=pltpu.VMEM)
        for n in range(n_in)
    ]
    return pl.pallas_call(
        body,
        out_shape=outs,
        in_specs=specs,
        out_specs=[pl.BlockSpec(memory_space=pltpu.VMEM) for _ in outs],
        scratch_shapes=scratch,
        name=name,
        compiler_params=pltpu.CompilerParams(vmem_limit_bytes=24 << 20),
        cost_estimate=pl.CostEstimate(flops=flops, bytes_accessed=nbytes, transcendentals=0),
    )


def on_device(patches, cand, offs, pairs, start):
    flat = pltpu.VMEM((16, VT), F32)
    xa, xb = call(pack_cols, [shape(X_ROWS, PATCH, dtype=BF)] * 2, [flat], "pack_cols", 1 << 20, n_in=2)(
        patches, start
    )
    xa = swapped(xa, "tile", col_a)
    xb = swapped(xb, "tile", col_b)
    ra, rb = call(pack_rows, [shape(R_ROWS, PATCH, dtype=BF)] * 2, [flat], "pack_rows", 1 << 20, n_in=4)(
        patches, start, xa, xb
    )
    ra = swapped(ra, "tile", row_a)
    rb = swapped(rb, "tile", row_b)
    sa, sb = call(
        pack_stack, [shape(S_ROWS, PATCH, dtype=BF)] * 2, [flat], "pack_stack", 1 << 20, smem=(3,), n_in=9
    )(patches, cand, offs, pairs, start, xa, xb, ra, rb)
    sa = swapped(sa, "stack", stack_a)
    sb = swapped(sb, "stack", stack_b)
    halos = [pltpu.VMEM((X_ROWS, PATCH), BF)] * 2 + [pltpu.VMEM((R_ROWS, PATCH), BF)] * 2
    p0, p1 = call(own_targets, [shape(SEC, 2, VT)] * 2, halos, "own_targets", 1 << 31, n_in=7)(
        patches, cand, offs, xa, xb, ra, rb
    )
    targets, u1, t0, t1, c0, c1 = call(
        first_round,
        [shape(SEC, 2, 2, VT), shape(16, VT)] + [shape(24, VT)] * 4,
        halos + [pltpu.VMEM((S_ROWS, PATCH), BF)] * 2 + [pltpu.VMEM((24, VT), F32)],
        "first_round",
        1 << 30,
        smem=(3,),
        n_in=13,
    )(patches, cand, offs, pairs, start, xa, xb, ra, rb, sa, sb, p0, p1)
    moved = [
        swapped(u1, axis, partner)
        for axis, partner in (
            ("tile", col_a), ("tile", col_b), ("tile", row_a), ("tile", row_b), ("stack", stack_a), ("stack", stack_b),
        )
    ]
    (aligned,) = call(
        second_round, [shape(SEC, 2, VT)], [pltpu.VMEM((24, VT), F32)], "second_round", 1 << 20, n_in=11
    )(u1, *moved, t0, t1, c0, c1)
    return aligned, targets


def solution(mesh):
    placed = (
        P("stack", "tile", None),
        P("stack", None, None, "tile"),
        P("stack", None, None, None, "tile"),
        P("stack", None),
        P("stack", None, "tile"),
    )
    return jax.shard_map(
        on_device,
        mesh=mesh,
        in_specs=placed,
        out_specs=(P("stack", None, "tile"), P("stack", None, None, "tile")),
        check_vma=False,
    )
```

```python
import jax
import jax.numpy as jnp
from jax import lax
from jax.experimental import pallas as pl
from jax.experimental.pallas import tpu as pltpu
from jax.sharding import PartitionSpec as P

SIDE = 16
COLS = 4
PATCH = 128
VT = 256
HALF = 128
SEC = 8
PITCH = 128.0
STEP = 0.1
BF = jnp.bfloat16
F32 = jnp.float32
I32 = jnp.int32

X_ROWS = 8 * 32 + 64
C_ROWS = 64 + 32
S_ROWS = 736
CROSS = ((6, 1), (7, 0), (7, 1))


def swapped(block, axis, partner):
    return lax.ppermute(block, axis, [(i, partner(i)) for i in range(lax.axis_size(axis))])


def col_a(i):
    return i ^ 1


def col_b(i):
    return i // COLS * COLS + (COLS - 1 - i % COLS)


def row_a(i):
    return i ^ COLS


def row_b(i):
    return (COLS - 1 - i // COLS) * COLS + i % COLS


def stack_a(i):
    return i ^ 1


def stack_b(i):
    return (((i + 1) ^ 1) - 1) % 16


def tile_place():
    tile = lax.axis_index("tile").astype(I32)
    return tile // COLS, tile % COLS


def iota(shape, dim):
    return lax.broadcasted_iota(I32, shape, dim)


def two_parts(u):
    hi = u.astype(BF)
    return hi, (u - hi.astype(F32)).astype(BF)


def rows_of(start_ref, scr, first=0):
    for s in range(SEC):
        scr[first + 2 * s : first + 2 * s + 2, :] = start_ref[s]


def dot(a, b):
    return lax.dot_general(a, b, (((1,), (0,)), ((), ())), preferred_element_type=F32)


def dot_t(a, b):
    return lax.dot_general(a, b, (((1,), (1,)), ((), ())), preferred_element_type=F32)


def pack_first(
    patches, cand, offs, pairs, start, ra, rb, xa, xb, lower,
    scr, held, held_c, held_o, held_p, held_u, sems,
):
    sources = [(start, held_u), (pairs, held_p), (cand.at[6:8], held_c), (offs.at[6:8], held_o)]
    sources += [(patches.at[s : s + 8], held.at[s : s + 8]) for s in range(0, SEC, 8)]
    copies = [pltpu.make_async_copy(src, dst, sems.at[n]) for n, (src, dst) in enumerate(sources)]
    for copy in copies:
        copy.start()
    row, col = tile_place()
    off_a = jnp.where(col % 2 == 0, SIDE - 2, 0)
    j = iota((64, VT), 0)
    v = iota((64, VT), 1)
    off = jnp.where(j < 32, off_a, SIDE - 2 - off_a)
    source = (j % SIDE) * SIDE + off + (j % 32) // SIDE
    pick = (v == source).astype(BF)
    for copy in copies[:4]:
        copy.wait()
    rows_of(held_u, scr)
    hi, lo = two_parts(scr[...])
    for n, part in enumerate((hi[:, :HALF], hi[:, HALF:], lo[:, :HALF], lo[:, HALF:])):
        xa[256 + 16 * n : 272 + 16 * n, :] = part
        xb[256 + 16 * n : 272 + 16 * n, :] = part
    r = iota((16, HALF), 0)
    tied = jnp.zeros((16, HALF), F32)
    for p, (s, z) in enumerate(CROSS):
        lr, lc = local_place(held_c[s - 6, z], row, col)
        for n, plane in enumerate((lr, lc, held_o[s - 6, z, 0], held_o[s - 6, z, 1])):
            at = 512 + 64 * p + 16 * n
            plane = plane.astype(F32)
            lower[at : at + 16, :] = jnp.concatenate([plane[:, :HALF], plane[:, HALF:]], axis=0).astype(BF)
        tied = jnp.where(r == p, held_p[z : z + 1, s : s + 1].astype(F32), tied)
    lower[704:720, :] = tied.astype(BF)
    h, low = two_parts(scr[12:16, :])
    h, low = h.astype(F32), low.astype(F32)
    lower[720:736, :] = jnp.concatenate(
        [h[:, :HALF], h[:, HALF:], low[:, :HALF], low[:, HALF:]], axis=0
    ).astype(BF)
    first = jnp.where(row % 2 == 0, VT - 32, 0)
    for s in range(SEC):
        if s % 8 == 0:
            copies[4 + s // 8].wait()
        strips = dot(pick, held[s]).astype(BF)
        xa[s * 32 : s * 32 + 32, :] = strips[:32]
        xb[s * 32 : s * 32 + 32, :] = strips[32:]
        ra[s] = held[s, pl.ds(pl.multiple_of(first, 32), 32), :]
        rb[s] = held[s, pl.ds(pl.multiple_of(VT - 32 - first, 32), 32), :]
        if s >= 6:
            lower[(s - 6) * 256 : (s - 5) * 256, :] = held[s]


def pack_corners(start, xa, xb, ca, cb, scr):
    row, col = tile_place()
    off_a = jnp.where(row % 2 == 0, SIDE - 2, 0)
    both = jnp.concatenate([xa[0:256, :], xb[0:256, :]], axis=0)
    q = iota((128, 512), 0)
    k = iota((128, 512), 1)
    off = jnp.where(q < 64, off_a, SIDE - 2 - off_a)
    side = (q % 8) // 4
    buffer = jnp.where(col % 2 == 0, 1 - side, side)
    source = buffer * 256 + (q % 64) // 8 * 32 + (q % 4) // 2 * SIDE + off + q % 2
    corners = dot((k == source).astype(BF), both).astype(BF)
    ca[0:64, :] = corners[:64]
    cb[0:64, :] = corners[64:]
    rows_of(start, scr)
    hi, lo = two_parts(scr[...])
    even = row % 2 == 0
    for out, second in ((ca, even), (cb, jnp.logical_not(even))):

        @pl.when(second)
        def _():
            out[64:80, :] = hi[:, HALF:]
            out[80:96, :] = lo[:, HALF:]

        @pl.when(jnp.logical_not(second))
        def _():
            out[64:80, :] = hi[:, :HALF]
            out[80:96, :] = lo[:, :HALF]


def local_place(ids, row, col):
    tile = ids >> 8
    lr = (tile >> 2) * SIDE + ((ids >> 4) & 15) - row * SIDE
    lc = (tile & 3) * SIDE + (ids & 15) - col * SIDE
    return lr, lc


def picked(scores, slot, sub, vregs, score):
    for n, at in enumerate(vregs):
        got = jnp.take_along_axis(scores[at : at + 8], sub, axis=0)
        score = jnp.where(slot == n, got, score)
    return score


def inner_half(h, mine, own, left, right, lr, lc):
    table = jnp.concatenate([own[0:160] if h == 0 else own[96:256], left, right], axis=0)
    scores = dot_t(table, mine)
    i = lr if h == 0 else lr - 6
    outside_c = (lc < 0) | (lc >= SIDE)
    side = jnp.where(lc >= SIDE, 1, 0)
    slot = jnp.where(outside_c, 20 + side * 4 + (lc & 1) * 2 + (lr >> 3), i * 2 + (lc >> 3))
    slot = jnp.where((lr < 0) | (lr >= SIDE), -1, slot)
    sub = jnp.where(outside_c, lr & 7, lc & 7)
    return picked(scores, slot, sub, range(0, 224, 8), jnp.zeros((8, HALF), F32))


def half_targets(h, mine, score, strip, corner, lr, lc, off_r, off_c):
    rows, first = corner
    scores = dot_t(jnp.concatenate([strip, rows], axis=0), mine)
    outside_c = (lc < 0) | (lc >= SIDE)
    side = jnp.where(lc >= SIDE, 1, 0)
    beyond = lr < 0 if h == 0 else lr >= SIDE
    slot = jnp.where(outside_c, 4, (lr & 1) * 2 + (lc >> 3))
    slot = jnp.where(beyond, slot, -1)
    sub = jnp.where(outside_c, side * 4 + (lc & 1) * 2 + (lr & 1), lc & 7)
    score = picked(scores, slot, sub, (0, 8, 16, 24, 32 + first), score)
    score = score * PATCH ** (-0.5)
    e = jnp.exp(score - jnp.max(score, axis=0, keepdims=True))
    lane = iota((8, HALF), 1)
    step_r = (lr - (lane >> 4) - 8 * h).astype(F32) + off_r * (1.0 / PITCH)
    step_c = (lc - (lane & 15)).astype(F32) + off_c * (1.0 / PITCH)
    total = jnp.sum(e, axis=0, keepdims=True)
    t_r = jnp.sum(e * step_r, axis=0, keepdims=True) / total
    t_c = jnp.sum(e * step_c, axis=0, keepdims=True) / total
    return jnp.concatenate([t_r, t_c], axis=0)


def lower_planes(lower, p):
    return [lower[512 + 64 * p + 16 * n : 528 + 64 * p + 16 * n, :].astype(F32) for n in range(4)]


def inner_scores(patches, cand, xa, xb, lower, inner, left, right):
    row, col = tile_place()
    sort_halos(col, left, right, xa, xb)

    def sides(d):
        at = slice(d * 32, d * 32 + 32)
        return patches[d], left[at, :], right[at, :]

    def one(s, z):
        pieces = sides(s + z + 1)
        for h in range(2):
            lanes = slice(h * HALF, h * HALF + HALF)
            lr, lc = local_place(cand[s, z, :, lanes], row, col)
            inner[z, s, h] = inner_half(h, patches[s, lanes, :], *pieces, lr, lc)

    for s in range(SEC - 1):
        one(s, 0)
        if s < SEC - 2:
            one(s, 1)
    for p, (s, z) in enumerate(CROSS):
        pieces = sides(s + z + 1 - SEC)
        planes = lower_planes(lower, p)
        for h in range(2):
            mine = lower[256 * (s - 6) + HALF * h : 256 * (s - 6) + HALF * h + HALF, :]
            lr, lc = [plane[8 * h : 8 * h + 8].astype(I32) for plane in planes[:2]]
            inner[z, s + 2, h] = inner_half(h, mine, *pieces, lr, lc)


def lower_targets(start, ra, rb, ca, cb, lower, inner, sent):
    row, _ = tile_place()
    even = row % 2 == 0

    def pick(p, q, at):
        return jnp.where(even, q[at], p[at]), jnp.where(even, p[at], q[at])

    strips = [pick(ra, rb, d) for d in range(2)]
    corners = pick(ca, cb, slice(0, 16))
    for p, (s, z) in enumerate(CROSS):
        d = s + z + 1 - SEC
        mine = lower[256 * (s - 6) : 256 * (s - 6) + 256, :]
        planes = lower_planes(lower, p)
        for h in range(2):
            lanes = slice(h * HALF, h * HALF + HALF)
            lr, lc, off_r, off_c = [plane[8 * h : 8 * h + 8] for plane in planes]
            sent[2 * p : 2 * p + 2, lanes] = half_targets(
                h, mine[lanes, :], inner[z, s + 2, h], strips[d][h], (corners[h], 8 * d),
                lr.astype(I32), lc.astype(I32), off_r, off_c,
            )
    sent[6:8, :] = start[0]
    sent[8:10, :] = start[1]
    sent[10:16, :] = jnp.zeros((6, VT), F32)


def own_targets(
    patches, cand, offs, pairs, start, xa, xb, ra, rb, ca, cb, lower, inner, sent,
    p0, p1, u1, t0, t1, c0, c1, cross, low,
    left, right, above, below, top, bottom, tall,
):
    row, col = tile_place()
    stack = lax.axis_index("stack").astype(I32)
    sort_halos(col, left, right, xa, xb)
    sort_halos(row, above, below, ra, rb)
    sort_halos(row, top, bottom, ca, cb)

    def one(s, z, store, corner_first):
        d = s + z + 1

        for h in range(2):
            strip, src = (above, top) if h == 0 else (below, bottom)
            at = slice(d // 2 * 16, d // 2 * 16 + 16)
            lanes = slice(h * HALF, h * HALF + HALF)
            lr, lc = local_place(cand[s, z, :, lanes], row, col)
            store[s, :, lanes] = half_targets(
                h, patches[s, lanes, :], inner[z, s, h], strip[d], (src[at, :], corner_first), lr, lc,
                offs[s, z, 0, :, lanes].astype(F32), offs[s, z, 1, :, lanes].astype(F32),
            )

    for s in range(SEC - 1):
        one(s, 0, p0, 8 * ((s + 1) % 2))
        if s < SEC - 2:
            one(s, 1, p1, 8 * (s % 2))

    nothing = jnp.zeros((2, VT), F32)
    p0[7] = nothing
    p1[6] = nothing
    p1[7] = nothing

    tied = jnp.where(stack == 0, 0.0, lower[704:720, :].astype(F32))
    last = stack == lax.axis_size("stack") - 1
    for z, p, t, c in ((0, p0, t0, c0), (1, p1, t1, c1)):
        rows_of(p, t, 4)
        t[0:4, :] = jnp.zeros((4, VT), F32)
        c[0:4, :] = jnp.zeros((4, VT), F32)
        for s in range(SEC):
            here = jnp.full((2, VT), pairs[z, s], I32).astype(F32)
            if (s, z) in CROSS:
                n = CROSS.index((s, z))
                cross[2 * n : 2 * n + 2, :] = jnp.where(last, 0.0, here)
                here = nothing
            c[4 + 2 * s : 6 + 2 * s, :] = here
    cross[6:8, :] = nothing
    for p, (s, z) in enumerate(CROSS):
        t, c = ((t0, c0), (t1, c1))[z]
        at = 2 * (s - 6)
        t[at : at + 2, :] = sent[2 * p : 2 * p + 2, :]
        line = tied[p : p + 1, :]
        c[at : at + 2, :] = jnp.broadcast_to(jnp.concatenate([line, line], axis=1), (2, VT))
    ends = lower[720:736, :].astype(F32)
    tall[0:4, 0:HALF] = ends[0:4] + ends[8:12]
    tall[0:4, HALF:VT] = ends[4:8] + ends[12:16]
    rows_of(start, tall, 4)
    tall[20:24, :] = jnp.zeros((4, VT), F32)
    u = tall[4:20, :]

    def whole(ref):
        part = [ref[256 + 16 * n : 272 + 16 * n, :].astype(F32) for n in range(4)]
        return jnp.concatenate([part[0] + part[2], part[1] + part[3]], axis=1)

    def half(ref):
        part = ref[64:80, :].astype(F32) + ref[80:96, :].astype(F32)
        return jnp.concatenate([part, part], axis=1)

    plane = laplace(u, whole(left), whole(right), half(top), half(bottom), row, col)
    u1[...] = relaxed(u, tall, t0, t1, c0, c1, plane)
    base, own = tall[0:4, :], tall[4:8, :]
    near = jnp.concatenate([own[0:2], own[0:2]], axis=0)
    far = jnp.concatenate([jnp.zeros((2, VT), F32), own[2:4]], axis=0)
    got0 = jnp.concatenate([sent[0:2, :], sent[2:4, :]], axis=0)
    got1 = jnp.concatenate([nothing, sent[4:6, :]], axis=0)
    tied0 = jnp.concatenate([c1[0:2, :], c0[2:4, :]], axis=0)
    tied1 = jnp.concatenate([nothing, c1[2:4, :]], axis=0)
    low[0:4, :] = STEP * (tied0 * (near - base - got0) + tied1 * (far - base - got1))
    low[4:8, :] = jnp.zeros((4, VT), F32)


def sort_halos(index, first, second, p, q):
    @pl.when(index % 2 == 0)
    def _():
        first[...] = q[...]
        second[...] = p[...]

    @pl.when(index % 2 == 1)
    def _():
        first[...] = p[...]
        second[...] = q[...]


def laplace(u, left, right, above, below, row, col):
    lane = iota(u.shape, 1)
    b = lane & 15
    up = jnp.where(lane < SIDE, pltpu.roll(above, SIDE, 1), pltpu.roll(u, SIDE, 1))
    up = jnp.where((lane < SIDE) & (row == 0), u, up)
    down = jnp.where(lane >= VT - SIDE, pltpu.roll(below, VT - SIDE, 1), pltpu.roll(u, VT - SIDE, 1))
    down = jnp.where((lane >= VT - SIDE) & (row == COLS - 1), u, down)
    west = jnp.where(b == 0, pltpu.roll(left, VT - SIDE + 1, 1), pltpu.roll(u, 1, 1))
    west = jnp.where((b == 0) & (col == 0), u, west)
    east = jnp.where(b == SIDE - 1, pltpu.roll(right, SIDE - 1, 1), pltpu.roll(u, VT - 1, 1))
    east = jnp.where((b == SIDE - 1) & (col == COLS - 1), u, east)
    return ((down - u) - (u - up)) + ((east - u) - (u - west))


def relaxed(u, tall, t0, t1, c0, c1, plane):
    base = tall[0:20, :]
    s0 = c0[0:20, :] * (tall[2:22, :] - base - t0[0:20, :])
    s1 = c1[0:20, :] * (tall[4:24, :] - base - t1[0:20, :])
    zforce = s0[4:20] - s0[2:18] + s1[4:20] - s1[0:16]
    return u + STEP * (plane + zforce)


def cross_force(u, upper, got, cross):
    near, far = upper[0:2], upper[2:4]
    six = cross[0:2, :] * (near - u[12:14] - got[0:2, :])
    seven = cross[2:4, :] * (near - u[14:16] - got[2:4, :]) + cross[4:6, :] * (far - u[14:16] - got[4:6, :])
    return jnp.concatenate([jnp.zeros((12, VT), F32), six, seven], axis=0)


def first_round(start, part, got, cross, u1):
    u0 = jnp.concatenate([jnp.zeros((12, VT), F32), start[6], start[7]], axis=0)
    u1[...] = part[...] + STEP * cross_force(u0, got[6:10, :], got, cross)


def all_targets(p0, p1, got, targets):
    stack = lax.axis_index("stack").astype(I32)
    last = stack == lax.axis_size("stack") - 1
    for s in range(SEC):
        for z, p in ((0, p0), (1, p1)):
            if (s, z) in CROSS:
                n = CROSS.index((s, z))
                targets[s, z] = jnp.where(last, 0.0, got[2 * n : 2 * n + 2, :])
            else:
                targets[s, z] = p[s]


def second_round(u1, sa, sb, xa, xb, ra, rb, t0, t1, c0, c1, cross, low, got, out, tall):
    row, col = tile_place()
    stack = lax.axis_index("stack").astype(I32)
    col_even, row_even, stack_even = col % 2 == 0, row % 2 == 0, stack % 2 == 0
    u = u1[...]
    tall[4:20, :] = u
    below_rows = jnp.where(stack_even, sb[12:16, :], sa[12:16, :])
    upper = jnp.where(stack_even, sa[0:4, :], sb[0:4, :])
    tall[0:4, :] = below_rows + low[0:4, :]
    tall[20:24, :] = jnp.zeros((4, VT), F32)
    plane = laplace(
        u,
        jnp.where(col_even, xb[...], xa[...]),
        jnp.where(col_even, xa[...], xb[...]),
        jnp.where(row_even, rb[...], ra[...]),
        jnp.where(row_even, ra[...], rb[...]),
        row,
        col,
    )
    u = relaxed(u, tall, t0, t1, c0, c1, plane + cross_force(u, upper, got, cross))
    for s in range(SEC):
        out[s] = u[2 * s : 2 * s + 2]


def shape(*dims, dtype=F32):
    return jax.ShapeDtypeStruct(dims, dtype)


def call(body, outs, scratch, flops, n_in, smem=(), far=(), vmem=24 << 20):
    def space(n):
        return pltpu.SMEM if n in smem else pltpu.HBM if n in far else pltpu.VMEM

    return pl.pallas_call(
        body,
        out_shape=outs,
        in_specs=[pl.BlockSpec(memory_space=space(n)) for n in range(n_in)],
        out_specs=[pl.BlockSpec(memory_space=pltpu.VMEM) for _ in outs],
        scratch_shapes=scratch,
        name=body.__name__,
        compiler_params=pltpu.CompilerParams(vmem_limit_bytes=vmem),
        cost_estimate=pl.CostEstimate(flops=flops, bytes_accessed=1 << 20, transcendentals=0),
    )


def on_device(patches, cand, offs, pairs, start):
    pairs = pairs.T
    flat = pltpu.VMEM((16, VT), F32)
    held = [
        pltpu.VMEM((SEC, VT, PATCH), BF),
        pltpu.VMEM((2, 2, 8, VT), I32),
        pltpu.VMEM((2, 2, 2, 8, VT), I32),
        pltpu.VMEM((2, SEC), I32),
        pltpu.VMEM((SEC, 2, VT), F32),
        pltpu.SemaphoreType.DMA((4 + SEC,)),
    ]
    outs = [shape(SEC, 32, PATCH, dtype=BF)] * 2 + [shape(X_ROWS, PATCH, dtype=BF)] * 2 + [shape(S_ROWS, PATCH, dtype=BF)]
    ra, rb, xa, xb, lower = call(pack_first, outs, [flat] + held, 1 << 20, 5, far=(0, 1, 2, 3, 4), vmem=62 << 20)(
        patches, cand, offs, pairs, start
    )
    ra = swapped(ra, "tile", row_a)
    rb = swapped(rb, "tile", row_b)
    xa = swapped(xa, "tile", col_a)
    xb = swapped(xb, "tile", col_b)
    lower = swapped(lower, "stack", lambda i: (i + 1) % 16)
    ca, cb = call(pack_corners, [shape(C_ROWS, PATCH, dtype=BF)] * 2, [flat], 1 << 20, 3)(start, xa, xb)
    ca = swapped(ca, "tile", row_a)
    cb = swapped(cb, "tile", row_b)
    halos = (xa, xb, ra, rb, ca, cb)
    (inner,) = call(
        inner_scores, [shape(2, SEC + 2, 2, 8, HALF)], [pltpu.VMEM((X_ROWS, PATCH), BF)] * 2, 1 << 31, 5
    )(patches, cand, xa, xb, lower)
    (sent,) = call(lower_targets, [shape(16, VT)], [], 1 << 20, 7)(start, ra, rb, ca, cb, lower, inner)
    got = swapped(sent, "stack", lambda i: (i - 1) % 16)
    p0, p1, part, t0, t1, c0, c1, cross, low = call(
        own_targets,
        [shape(SEC, 2, VT)] * 2 + [shape(16, VT)] + [shape(24, VT)] * 4 + [shape(8, VT)] * 2,
        [pltpu.VMEM(a.shape, BF) for a in halos] + [pltpu.VMEM((24, VT), F32)],
        1 << 31,
        14,
        smem=(3,),
    )(patches, cand, offs, pairs, start, *halos, lower, inner, sent)
    stacked = [swapped(part, "stack", stack_a), swapped(part, "stack", stack_b)]
    (u1,) = call(first_round, [shape(16, VT)], [], 1 << 16, 4)(start, part, got, cross)
    moved = [swapped(u1, "tile", partner) for partner in (col_a, col_b, row_a, row_b)]
    (targets,) = call(all_targets, [shape(SEC, 2, 2, VT)], [], 1 << 20, 3)(p0, p1, got)
    (aligned,) = call(second_round, [shape(SEC, 2, VT)], [pltpu.VMEM((24, VT), F32)], 1 << 20, 14)(
        u1, *stacked, *moved, t0, t1, c0, c1, cross, low, got
    )
    return aligned, targets


def solution(mesh):
    placed = (
        P("stack", "tile", None),
        P("stack", None, None, "tile"),
        P("stack", None, None, None, "tile"),
        P("stack", None),
        P("stack", None, "tile"),
    )
    return jax.shard_map(
        on_device,
        mesh=mesh,
        in_specs=placed,
        out_specs=(P("stack", None, "tile"), P("stack", None, None, "tile")),
        check_vma=False,
    )
```

```python
import jax
import jax.numpy as jnp
from jax import lax
from jax.experimental import pallas as pl
from jax.experimental.pallas import tpu as pltpu
from jax.sharding import PartitionSpec as P

SIDE = 16
COLS = 4
PATCH = 128
VT = 256
HALF = 128
SEC = 8
PITCH = 128.0
STEP = 0.1
BF = jnp.bfloat16
F32 = jnp.float32
I32 = jnp.int32

X_ROWS = 8 * 32 + 64
C_ROWS = 64 + 32
S_ROWS = 736
CROSS = ((6, 1), (7, 0), (7, 1))


def swapped(block, axis, partner):
    return lax.ppermute(block, axis, [(i, partner(i)) for i in range(lax.axis_size(axis))])


def col_a(i):
    return i ^ 1


def col_b(i):
    return i // COLS * COLS + (COLS - 1 - i % COLS)


def row_a(i):
    return i ^ COLS


def row_b(i):
    return (COLS - 1 - i // COLS) * COLS + i % COLS


def stack_a(i):
    return i ^ 1


def stack_b(i):
    return (((i + 1) ^ 1) - 1) % 16


def tile_place():
    tile = lax.axis_index("tile").astype(I32)
    return tile // COLS, tile % COLS


def iota(shape, dim):
    return lax.broadcasted_iota(I32, shape, dim)


def two_parts(u):
    hi = u.astype(BF)
    return hi, (u - hi.astype(F32)).astype(BF)


def rows_of(start_ref, scr, first=0):
    for s in range(SEC):
        scr[first + 2 * s : first + 2 * s + 2, :] = start_ref[s]


def dot(a, b):
    return lax.dot_general(a, b, (((1,), (0,)), ((), ())), preferred_element_type=F32)


def dot_t(a, b):
    return lax.dot_general(a, b, (((1,), (1,)), ((), ())), preferred_element_type=F32)


def pack_first(
    patches, cand, offs, pairs, start, rb, ra, xb, xa, lower,
    scr, held, held_c, held_o, held_p, held_u, sems,
):
    sources = [(start, held_u), (pairs, held_p), (cand.at[6:8], held_c), (offs.at[6:8], held_o)]
    sources += [(patches.at[s : s + 8], held.at[s : s + 8]) for s in range(0, SEC, 8)]
    copies = [pltpu.make_async_copy(src, dst, sems.at[n]) for n, (src, dst) in enumerate(sources)]
    for copy in copies:
        copy.start()
    row, col = tile_place()
    off_a = jnp.where(col % 2 == 0, SIDE - 2, 0)
    j = iota((64, VT), 0)
    v = iota((64, VT), 1)
    off = jnp.where(j < 32, off_a, SIDE - 2 - off_a)
    source = (j % SIDE) * SIDE + off + (j % 32) // SIDE
    pick = (v == source).astype(BF)
    for copy in copies[:4]:
        copy.wait()
    rows_of(held_u, scr)
    hi, lo = two_parts(scr[...])
    for n, part in enumerate((hi[:, :HALF], hi[:, HALF:], lo[:, :HALF], lo[:, HALF:])):
        xa[256 + 16 * n : 272 + 16 * n, :] = part
        xb[256 + 16 * n : 272 + 16 * n, :] = part
    r = iota((16, HALF), 0)
    tied = jnp.zeros((16, HALF), F32)
    for p, (s, z) in enumerate(CROSS):
        lr, lc = local_place(held_c[s - 6, z], row, col)
        for n, plane in enumerate((lr, lc, held_o[s - 6, z, 0], held_o[s - 6, z, 1])):
            at = 512 + 64 * p + 16 * n
            plane = plane.astype(F32)
            lower[at : at + 16, :] = jnp.concatenate([plane[:, :HALF], plane[:, HALF:]], axis=0).astype(BF)
        tied = jnp.where(r == p, held_p[z : z + 1, s : s + 1].astype(F32), tied)
    lower[704:720, :] = tied.astype(BF)
    h, low = two_parts(scr[12:16, :])
    h, low = h.astype(F32), low.astype(F32)
    lower[720:736, :] = jnp.concatenate(
        [h[:, :HALF], h[:, HALF:], low[:, :HALF], low[:, HALF:]], axis=0
    ).astype(BF)
    first = jnp.where(row % 2 == 0, VT - 32, 0)
    for s in range(SEC):
        if s % 8 == 0:
            copies[4 + s // 8].wait()
        strips = dot(pick, held[s]).astype(BF)
        xa[s * 32 : s * 32 + 32, :] = strips[:32]
        xb[s * 32 : s * 32 + 32, :] = strips[32:]
        ra[s] = held[s, pl.ds(pl.multiple_of(first, 32), 32), :]
        rb[s] = held[s, pl.ds(pl.multiple_of(VT - 32 - first, 32), 32), :]
        if s >= 6:
            lower[(s - 6) * 256 : (s - 5) * 256, :] = held[s]


def pack_corners(start, xb, xa, cb, ca, scr):
    row, col = tile_place()
    off_a = jnp.where(row % 2 == 0, SIDE - 2, 0)
    both = jnp.concatenate([xa[0:256, :], xb[0:256, :]], axis=0)
    q = iota((128, 512), 0)
    k = iota((128, 512), 1)
    off = jnp.where(q < 64, off_a, SIDE - 2 - off_a)
    side = (q % 8) // 4
    buffer = jnp.where(col % 2 == 0, 1 - side, side)
    source = buffer * 256 + (q % 64) // 8 * 32 + (q % 4) // 2 * SIDE + off + q % 2
    corners = dot((k == source).astype(BF), both).astype(BF)
    ca[0:64, :] = corners[:64]
    cb[0:64, :] = corners[64:]
    rows_of(start, scr)
    hi, lo = two_parts(scr[...])
    even = row % 2 == 0
    for out, second in ((ca, even), (cb, jnp.logical_not(even))):

        @pl.when(second)
        def _():
            out[64:80, :] = hi[:, HALF:]
            out[80:96, :] = lo[:, HALF:]

        @pl.when(jnp.logical_not(second))
        def _():
            out[64:80, :] = hi[:, :HALF]
            out[80:96, :] = lo[:, :HALF]


def local_place(ids, row, col):
    tile = ids >> 8
    lr = (tile >> 2) * SIDE + ((ids >> 4) & 15) - row * SIDE
    lc = (tile & 3) * SIDE + (ids & 15) - col * SIDE
    return lr, lc


def picked(scores, slot, sub, vregs, score):
    for n, at in enumerate(vregs):
        got = jnp.take_along_axis(scores[at : at + 8], sub, axis=0)
        score = jnp.where(slot == n, got, score)
    return score


def inner_half(h, mine, own, left, right, lr, lc):
    table = jnp.concatenate([own[0:160] if h == 0 else own[96:256], left, right], axis=0)
    scores = dot_t(table, mine)
    i = lr if h == 0 else lr - 6
    outside_c = (lc < 0) | (lc >= SIDE)
    side = jnp.where(lc >= SIDE, 1, 0)
    slot = jnp.where(outside_c, 20 + side * 4 + (lc & 1) * 2 + (lr >> 3), i * 2 + (lc >> 3))
    slot = jnp.where((lr < 0) | (lr >= SIDE), -1, slot)
    sub = jnp.where(outside_c, lr & 7, lc & 7)
    return picked(scores, slot, sub, range(0, 224, 8), jnp.zeros((8, HALF), F32))


def half_targets(h, mine, score, strip, corner, lr, lc, off_r, off_c):
    rows, first = corner
    scores = dot_t(jnp.concatenate([strip, rows], axis=0), mine)
    outside_c = (lc < 0) | (lc >= SIDE)
    side = jnp.where(lc >= SIDE, 1, 0)
    beyond = lr < 0 if h == 0 else lr >= SIDE
    slot = jnp.where(outside_c, 4, (lr & 1) * 2 + (lc >> 3))
    slot = jnp.where(beyond, slot, -1)
    sub = jnp.where(outside_c, side * 4 + (lc & 1) * 2 + (lr & 1), lc & 7)
    score = picked(scores, slot, sub, (0, 8, 16, 24, 32 + first), score)
    score = score * PATCH ** (-0.5)
    e = jnp.exp(score - jnp.max(score, axis=0, keepdims=True))
    lane = iota((8, HALF), 1)
    step_r = (lr - (lane >> 4) - 8 * h).astype(F32) + off_r * (1.0 / PITCH)
    step_c = (lc - (lane & 15)).astype(F32) + off_c * (1.0 / PITCH)
    total = jnp.sum(e, axis=0, keepdims=True)
    t_r = jnp.sum(e * step_r, axis=0, keepdims=True) / total
    t_c = jnp.sum(e * step_c, axis=0, keepdims=True) / total
    return jnp.concatenate([t_r, t_c], axis=0)


def lower_planes(lower, p):
    return [lower[512 + 64 * p + 16 * n : 528 + 64 * p + 16 * n, :].astype(F32) for n in range(4)]


def inner_scores(patches, cand, xb, xa, lower, inner, left, right):
    row, col = tile_place()
    sort_halos(col, left, right, xa, xb)

    def sides(d):
        at = slice(d * 32, d * 32 + 32)
        return patches[d], left[at, :], right[at, :]

    def one(s, z):
        pieces = sides(s + z + 1)
        for h in range(2):
            lanes = slice(h * HALF, h * HALF + HALF)
            lr, lc = local_place(cand[s, z, :, lanes], row, col)
            inner[z, s, h] = inner_half(h, patches[s, lanes, :], *pieces, lr, lc)

    for s in range(SEC - 1):
        one(s, 0)
        if s < SEC - 2:
            one(s, 1)
    for p, (s, z) in enumerate(CROSS):
        pieces = sides(s + z + 1 - SEC)
        planes = lower_planes(lower, p)
        for h in range(2):
            mine = lower[256 * (s - 6) + HALF * h : 256 * (s - 6) + HALF * h + HALF, :]
            lr, lc = [plane[8 * h : 8 * h + 8].astype(I32) for plane in planes[:2]]
            inner[z, s + 2, h] = inner_half(h, mine, *pieces, lr, lc)


def lower_targets(start, rb, ra, cb, ca, lower, inner, sent):
    row, _ = tile_place()
    even = row % 2 == 0

    def pick(p, q, at):
        return jnp.where(even, q[at], p[at]), jnp.where(even, p[at], q[at])

    strips = [pick(ra, rb, d) for d in range(2)]
    corners = pick(ca, cb, slice(0, 16))
    for p, (s, z) in enumerate(CROSS):
        d = s + z + 1 - SEC
        mine = lower[256 * (s - 6) : 256 * (s - 6) + 256, :]
        planes = lower_planes(lower, p)
        for h in range(2):
            lanes = slice(h * HALF, h * HALF + HALF)
            lr, lc, off_r, off_c = [plane[8 * h : 8 * h + 8] for plane in planes]
            sent[2 * p : 2 * p + 2, lanes] = half_targets(
                h, mine[lanes, :], inner[z, s + 2, h], strips[d][h], (corners[h], 8 * d),
                lr.astype(I32), lc.astype(I32), off_r, off_c,
            )
    sent[6:8, :] = start[0]
    sent[8:10, :] = start[1]
    sent[10:16, :] = jnp.zeros((6, VT), F32)


def own_targets(
    patches, cand, offs, pairs, start, xb, xa, rb, ra, cb, ca, lower, inner, sent,
    p0, p1, u1, t0, t1, c0, c1, cross, low,
    left, right, above, below, top, bottom, tall,
):
    row, col = tile_place()
    stack = lax.axis_index("stack").astype(I32)
    sort_halos(col, left, right, xa, xb)
    sort_halos(row, above, below, ra, rb)
    sort_halos(row, top, bottom, ca, cb)

    def one(s, z, store, corner_first):
        d = s + z + 1

        for h in range(2):
            strip, src = (above, top) if h == 0 else (below, bottom)
            at = slice(d // 2 * 16, d // 2 * 16 + 16)
            lanes = slice(h * HALF, h * HALF + HALF)
            lr, lc = local_place(cand[s, z, :, lanes], row, col)
            store[s, :, lanes] = half_targets(
                h, patches[s, lanes, :], inner[z, s, h], strip[d], (src[at, :], corner_first), lr, lc,
                offs[s, z, 0, :, lanes].astype(F32), offs[s, z, 1, :, lanes].astype(F32),
            )

    for s in range(SEC - 1):
        one(s, 0, p0, 8 * ((s + 1) % 2))
        if s < SEC - 2:
            one(s, 1, p1, 8 * (s % 2))

    nothing = jnp.zeros((2, VT), F32)
    p0[7] = nothing
    p1[6] = nothing
    p1[7] = nothing

    tied = jnp.where(stack == 0, 0.0, lower[704:720, :].astype(F32))
    last = stack == lax.axis_size("stack") - 1
    for z, p, t, c in ((0, p0, t0, c0), (1, p1, t1, c1)):
        rows_of(p, t, 4)
        t[0:4, :] = jnp.zeros((4, VT), F32)
        c[0:4, :] = jnp.zeros((4, VT), F32)
        for s in range(SEC):
            here = jnp.full((2, VT), pairs[z, s], I32).astype(F32)
            if (s, z) in CROSS:
                n = CROSS.index((s, z))
                cross[2 * n : 2 * n + 2, :] = jnp.where(last, 0.0, here)
                here = nothing
            c[4 + 2 * s : 6 + 2 * s, :] = here
    cross[6:8, :] = nothing
    for p, (s, z) in enumerate(CROSS):
        t, c = ((t0, c0), (t1, c1))[z]
        at = 2 * (s - 6)
        t[at : at + 2, :] = sent[2 * p : 2 * p + 2, :]
        line = tied[p : p + 1, :]
        c[at : at + 2, :] = jnp.broadcast_to(jnp.concatenate([line, line], axis=1), (2, VT))
    ends = lower[720:736, :].astype(F32)
    tall[0:4, 0:HALF] = ends[0:4] + ends[8:12]
    tall[0:4, HALF:VT] = ends[4:8] + ends[12:16]
    rows_of(start, tall, 4)
    tall[20:24, :] = jnp.zeros((4, VT), F32)
    u = tall[4:20, :]

    def whole(ref):
        part = [ref[256 + 16 * n : 272 + 16 * n, :].astype(F32) for n in range(4)]
        return jnp.concatenate([part[0] + part[2], part[1] + part[3]], axis=1)

    def half(ref):
        part = ref[64:80, :].astype(F32) + ref[80:96, :].astype(F32)
        return jnp.concatenate([part, part], axis=1)

    plane = laplace(u, whole(left), whole(right), half(top), half(bottom), row, col)
    u1[...] = relaxed(u, tall, t0, t1, c0, c1, plane)
    base, own = tall[0:4, :], tall[4:8, :]
    near = jnp.concatenate([own[0:2], own[0:2]], axis=0)
    far = jnp.concatenate([jnp.zeros((2, VT), F32), own[2:4]], axis=0)
    got0 = jnp.concatenate([sent[0:2, :], sent[2:4, :]], axis=0)
    got1 = jnp.concatenate([nothing, sent[4:6, :]], axis=0)
    tied0 = jnp.concatenate([c1[0:2, :], c0[2:4, :]], axis=0)
    tied1 = jnp.concatenate([nothing, c1[2:4, :]], axis=0)
    low[0:4, :] = STEP * (tied0 * (near - base - got0) + tied1 * (far - base - got1))
    low[4:8, :] = jnp.zeros((4, VT), F32)


def sort_halos(index, first, second, p, q):
    @pl.when(index % 2 == 0)
    def _():
        first[...] = q[...]
        second[...] = p[...]

    @pl.when(index % 2 == 1)
    def _():
        first[...] = p[...]
        second[...] = q[...]


def laplace(u, left, right, above, below, row, col):
    lane = iota(u.shape, 1)
    b = lane & 15
    up = jnp.where(lane < SIDE, pltpu.roll(above, SIDE, 1), pltpu.roll(u, SIDE, 1))
    up = jnp.where((lane < SIDE) & (row == 0), u, up)
    down = jnp.where(lane >= VT - SIDE, pltpu.roll(below, VT - SIDE, 1), pltpu.roll(u, VT - SIDE, 1))
    down = jnp.where((lane >= VT - SIDE) & (row == COLS - 1), u, down)
    west = jnp.where(b == 0, pltpu.roll(left, VT - SIDE + 1, 1), pltpu.roll(u, 1, 1))
    west = jnp.where((b == 0) & (col == 0), u, west)
    east = jnp.where(b == SIDE - 1, pltpu.roll(right, SIDE - 1, 1), pltpu.roll(u, VT - 1, 1))
    east = jnp.where((b == SIDE - 1) & (col == COLS - 1), u, east)
    return ((down - u) - (u - up)) + ((east - u) - (u - west))


def relaxed(u, tall, t0, t1, c0, c1, plane):
    base = tall[0:20, :]
    s0 = c0[0:20, :] * (tall[2:22, :] - base - t0[0:20, :])
    s1 = c1[0:20, :] * (tall[4:24, :] - base - t1[0:20, :])
    zforce = s0[4:20] - s0[2:18] + s1[4:20] - s1[0:16]
    return u + STEP * (plane + zforce)


def cross_force(u, upper, got, cross):
    near, far = upper[0:2], upper[2:4]
    six = cross[0:2, :] * (near - u[12:14] - got[0:2, :])
    seven = cross[2:4, :] * (near - u[14:16] - got[2:4, :]) + cross[4:6, :] * (far - u[14:16] - got[4:6, :])
    return jnp.concatenate([jnp.zeros((12, VT), F32), six, seven], axis=0)


def first_round(start, part, got, cross, u1):
    u0 = jnp.concatenate([jnp.zeros((12, VT), F32), start[6], start[7]], axis=0)
    u1[...] = part[...] + STEP * cross_force(u0, got[6:10, :], got, cross)


def all_targets(p0, p1, got, targets):
    stack = lax.axis_index("stack").astype(I32)
    last = stack == lax.axis_size("stack") - 1
    for s in range(SEC):
        for z, p in ((0, p0), (1, p1)):
            if (s, z) in CROSS:
                n = CROSS.index((s, z))
                targets[s, z] = jnp.where(last, 0.0, got[2 * n : 2 * n + 2, :])
            else:
                targets[s, z] = p[s]


def second_round(u1, sb, sa, xa, xb, ra, rb, t0, t1, c0, c1, cross, low, got, out, tall):
    row, col = tile_place()
    stack = lax.axis_index("stack").astype(I32)
    col_even, row_even, stack_even = col % 2 == 0, row % 2 == 0, stack % 2 == 0
    u = u1[...]
    tall[4:20, :] = u
    below_rows = jnp.where(stack_even, sb[12:16, :], sa[12:16, :])
    upper = jnp.where(stack_even, sa[0:4, :], sb[0:4, :])
    tall[0:4, :] = below_rows + low[0:4, :]
    tall[20:24, :] = jnp.zeros((4, VT), F32)
    plane = laplace(
        u,
        jnp.where(col_even, xb[...], xa[...]),
        jnp.where(col_even, xa[...], xb[...]),
        jnp.where(row_even, rb[...], ra[...]),
        jnp.where(row_even, ra[...], rb[...]),
        row,
        col,
    )
    u = relaxed(u, tall, t0, t1, c0, c1, plane + cross_force(u, upper, got, cross))
    for s in range(SEC):
        out[s] = u[2 * s : 2 * s + 2]


def shape(*dims, dtype=F32):
    return jax.ShapeDtypeStruct(dims, dtype)


def call(body, outs, scratch, flops, n_in, smem=(), far=(), vmem=24 << 20):
    def space(n):
        return pltpu.SMEM if n in smem else pltpu.HBM if n in far else pltpu.VMEM

    return pl.pallas_call(
        body,
        out_shape=outs,
        in_specs=[pl.BlockSpec(memory_space=space(n)) for n in range(n_in)],
        out_specs=[pl.BlockSpec(memory_space=pltpu.VMEM) for _ in outs],
        scratch_shapes=scratch,
        name=body.__name__,
        compiler_params=pltpu.CompilerParams(vmem_limit_bytes=vmem),
        cost_estimate=pl.CostEstimate(flops=flops, bytes_accessed=1 << 20, transcendentals=0),
    )


def on_device(patches, cand, offs, pairs, start):
    pairs = pairs.T
    flat = pltpu.VMEM((16, VT), F32)
    held = [
        pltpu.VMEM((SEC, VT, PATCH), BF),
        pltpu.VMEM((2, 2, 8, VT), I32),
        pltpu.VMEM((2, 2, 2, 8, VT), I32),
        pltpu.VMEM((2, SEC), I32),
        pltpu.VMEM((SEC, 2, VT), F32),
        pltpu.SemaphoreType.DMA((4 + SEC,)),
    ]
    outs = [shape(SEC, 32, PATCH, dtype=BF)] * 2 + [shape(X_ROWS, PATCH, dtype=BF)] * 2 + [shape(S_ROWS, PATCH, dtype=BF)]
    rb, ra, xb, xa, lower = call(pack_first, outs, [flat] + held, 1 << 20, 5, far=(0, 1, 2, 3, 4), vmem=62 << 20)(
        patches, cand, offs, pairs, start
    )
    rb = swapped(rb, "tile", row_b)
    ra = swapped(ra, "tile", row_a)
    xa = swapped(xa, "tile", col_a)
    xb = swapped(xb, "tile", col_b)
    lower = swapped(lower, "stack", lambda i: (i + 1) % 16)
    cb, ca = call(pack_corners, [shape(C_ROWS, PATCH, dtype=BF)] * 2, [flat], 1 << 20, 3)(start, xb, xa)
    cb = swapped(cb, "tile", row_b)
    ca = swapped(ca, "tile", row_a)
    halos = (xb, xa, rb, ra, cb, ca)
    (inner,) = call(
        inner_scores, [shape(2, SEC + 2, 2, 8, HALF)], [pltpu.VMEM((X_ROWS, PATCH), BF)] * 2, 1 << 31, 5
    )(patches, cand, xb, xa, lower)
    (sent,) = call(lower_targets, [shape(16, VT)], [], 1 << 20, 7)(start, rb, ra, cb, ca, lower, inner)
    got = swapped(sent, "stack", lambda i: (i - 1) % 16)
    p0, p1, part, t0, t1, c0, c1, cross, low = call(
        own_targets,
        [shape(SEC, 2, VT)] * 2 + [shape(16, VT)] + [shape(24, VT)] * 4 + [shape(8, VT)] * 2,
        [pltpu.VMEM(a.shape, BF) for a in halos] + [pltpu.VMEM((24, VT), F32)],
        1 << 31,
        14,
        smem=(3,),
    )(patches, cand, offs, pairs, start, *halos, lower, inner, sent)
    sa = swapped(part, "stack", stack_a)
    sb = swapped(part, "stack", stack_b)
    (u1,) = call(first_round, [shape(16, VT)], [], 1 << 16, 4)(start, part, got, cross)
    moved = [swapped(u1, "tile", partner) for partner in (col_a, col_b, row_a, row_b)]
    (targets,) = call(all_targets, [shape(SEC, 2, 2, VT)], [], 1 << 20, 3)(p0, p1, got)
    (aligned,) = call(second_round, [shape(SEC, 2, VT)], [pltpu.VMEM((24, VT), F32)], 1 << 20, 14)(
        u1, sb, sa, *moved, t0, t1, c0, c1, cross, low, got
    )
    return aligned, targets


def solution(mesh):
    placed = (
        P("stack", "tile", None),
        P("stack", None, None, "tile"),
        P("stack", None, None, None, "tile"),
        P("stack", None),
        P("stack", None, "tile"),
    )
    return jax.shard_map(
        on_device,
        mesh=mesh,
        in_specs=placed,
        out_specs=(P("stack", None, "tile"), P("stack", None, None, "tile")),
        check_vma=False,
    )
```

```python
import jax
import jax.numpy as jnp
from jax import lax
from jax.experimental import pallas as pl
from jax.experimental.pallas import tpu as pltpu
from jax.sharding import PartitionSpec as P

SIDE = 16
COLS = 4
PATCH = 128
VT = 256
HALF = 128
SEC = 8
PITCH = 128.0
STEP = 0.1
BF = jnp.bfloat16
F32 = jnp.float32
I32 = jnp.int32

X_ROWS = 8 * 32 + 64
C_ROWS = 64 + 32
S_ROWS = 736
CROSS = ((6, 1), (7, 0), (7, 1))


def swapped(block, axis, partner):
    return lax.ppermute(block, axis, [(i, partner(i)) for i in range(lax.axis_size(axis))])


def col_a(i):
    return i ^ 1


def col_b(i):
    return i // COLS * COLS + (COLS - 1 - i % COLS)


def row_a(i):
    return i ^ COLS


def row_b(i):
    return (COLS - 1 - i // COLS) * COLS + i % COLS


def stack_a(i):
    return i ^ 1


def stack_b(i):
    return (((i + 1) ^ 1) - 1) % 16


def tile_place():
    tile = lax.axis_index("tile").astype(I32)
    return tile // COLS, tile % COLS


def iota(shape, dim):
    return lax.broadcasted_iota(I32, shape, dim)


def two_parts(u):
    hi = u.astype(BF)
    return hi, (u - hi.astype(F32)).astype(BF)


def rows_of(start_ref, scr, first=0):
    for s in range(SEC):
        scr[first + 2 * s : first + 2 * s + 2, :] = start_ref[s]


def dot(a, b):
    return lax.dot_general(a, b, (((1,), (0,)), ((), ())), preferred_element_type=F32)


def dot_t(a, b):
    return lax.dot_general(a, b, (((1,), (1,)), ((), ())), preferred_element_type=F32)


def pack_first(
    patches, cand, offs, pairs, start, rb, ra, xb, xa, lower,
    scr, held, held_c, held_o, held_p, held_u, sems,
):
    sources = [(start, held_u), (pairs, held_p), (cand.at[6:8], held_c), (offs.at[6:8], held_o)]
    sources += [(patches.at[s : s + 8], held.at[s : s + 8]) for s in range(0, SEC, 8)]
    copies = [pltpu.make_async_copy(src, dst, sems.at[n]) for n, (src, dst) in enumerate(sources)]
    for copy in copies:
        copy.start()
    row, col = tile_place()
    off_a = jnp.where(col % 2 == 0, SIDE - 2, 0)
    j = iota((64, VT), 0)
    v = iota((64, VT), 1)
    off = jnp.where(j < 32, off_a, SIDE - 2 - off_a)
    source = (j % SIDE) * SIDE + off + (j % 32) // SIDE
    pick = (v == source).astype(BF)
    for copy in copies[:4]:
        copy.wait()
    rows_of(held_u, scr)
    hi, lo = two_parts(scr[...])
    for n, part in enumerate((hi[:, :HALF], hi[:, HALF:], lo[:, :HALF], lo[:, HALF:])):
        xa[256 + 16 * n : 272 + 16 * n, :] = part
        xb[256 + 16 * n : 272 + 16 * n, :] = part
    r = iota((16, HALF), 0)
    tied = jnp.zeros((16, HALF), F32)
    for p, (s, z) in enumerate(CROSS):
        lr, lc = local_place(held_c[s - 6, z], row, col)
        for n, plane in enumerate((lr, lc, held_o[s - 6, z, 0], held_o[s - 6, z, 1])):
            at = 512 + 64 * p + 16 * n
            plane = plane.astype(F32)
            lower[at : at + 16, :] = jnp.concatenate([plane[:, :HALF], plane[:, HALF:]], axis=0).astype(BF)
        tied = jnp.where(r == p, held_p[z : z + 1, s : s + 1].astype(F32), tied)
    lower[704:720, :] = tied.astype(BF)
    h, low = two_parts(scr[12:16, :])
    h, low = h.astype(F32), low.astype(F32)
    lower[720:736, :] = jnp.concatenate(
        [h[:, :HALF], h[:, HALF:], low[:, :HALF], low[:, HALF:]], axis=0
    ).astype(BF)
    first = jnp.where(row % 2 == 0, VT - 32, 0)
    for s in range(SEC):
        if s % 8 == 0:
            copies[4 + s // 8].wait()
        strips = dot(pick, held[s]).astype(BF)
        xa[s * 32 : s * 32 + 32, :] = strips[:32]
        xb[s * 32 : s * 32 + 32, :] = strips[32:]
        ra[s] = held[s, pl.ds(pl.multiple_of(first, 32), 32), :]
        rb[s] = held[s, pl.ds(pl.multiple_of(VT - 32 - first, 32), 32), :]
        if s >= 6:
            lower[(s - 6) * 256 : (s - 5) * 256, :] = held[s]


def pack_corners(start, xb, xa, cb, ca, scr):
    row, col = tile_place()
    off_a = jnp.where(row % 2 == 0, SIDE - 2, 0)
    both = jnp.concatenate([xa[0:256, :], xb[0:256, :]], axis=0)
    q = iota((128, 512), 0)
    k = iota((128, 512), 1)
    off = jnp.where(q < 64, off_a, SIDE - 2 - off_a)
    side = (q % 8) // 4
    buffer = jnp.where(col % 2 == 0, 1 - side, side)
    source = buffer * 256 + (q % 64) // 8 * 32 + (q % 4) // 2 * SIDE + off + q % 2
    corners = dot((k == source).astype(BF), both).astype(BF)
    ca[0:64, :] = corners[:64]
    cb[0:64, :] = corners[64:]
    rows_of(start, scr)
    hi, lo = two_parts(scr[...])
    even = row % 2 == 0
    for out, second in ((ca, even), (cb, jnp.logical_not(even))):

        @pl.when(second)
        def _():
            out[64:80, :] = hi[:, HALF:]
            out[80:96, :] = lo[:, HALF:]

        @pl.when(jnp.logical_not(second))
        def _():
            out[64:80, :] = hi[:, :HALF]
            out[80:96, :] = lo[:, :HALF]


def local_place(ids, row, col):
    tile = ids >> 8
    lr = (tile >> 2) * SIDE + ((ids >> 4) & 15) - row * SIDE
    lc = (tile & 3) * SIDE + (ids & 15) - col * SIDE
    return lr, lc


def picked(scores, slot, sub, vregs, score):
    for n, at in enumerate(vregs):
        got = jnp.take_along_axis(scores[at : at + 8], sub, axis=0)
        score = jnp.where(slot == n, got, score)
    return score


def inner_half(h, mine, own, left, right, lr, lc):
    table = jnp.concatenate([own[0:160] if h == 0 else own[96:256], left, right], axis=0)
    scores = dot_t(table, mine)
    i = lr if h == 0 else lr - 6
    outside_c = (lc < 0) | (lc >= SIDE)
    side = jnp.where(lc >= SIDE, 1, 0)
    slot = jnp.where(outside_c, 20 + side * 4 + (lc & 1) * 2 + (lr >> 3), i * 2 + (lc >> 3))
    slot = jnp.where((lr < 0) | (lr >= SIDE), -1, slot)
    sub = jnp.where(outside_c, lr & 7, lc & 7)
    return picked(scores, slot, sub, range(0, 224, 8), jnp.zeros((8, HALF), F32))


def half_targets(h, mine, score, strip, corner, lr, lc, off_r, off_c):
    rows, first = corner
    scores = dot_t(jnp.concatenate([strip, rows], axis=0), mine)
    outside_c = (lc < 0) | (lc >= SIDE)
    side = jnp.where(lc >= SIDE, 1, 0)
    beyond = lr < 0 if h == 0 else lr >= SIDE
    slot = jnp.where(outside_c, 4, (lr & 1) * 2 + (lc >> 3))
    slot = jnp.where(beyond, slot, -1)
    sub = jnp.where(outside_c, side * 4 + (lc & 1) * 2 + (lr & 1), lc & 7)
    score = picked(scores, slot, sub, (0, 8, 16, 24, 32 + first), score)
    score = score * PATCH ** (-0.5)
    e = jnp.exp(score - jnp.max(score, axis=0, keepdims=True))
    lane = iota((8, HALF), 1)
    step_r = (lr - (lane >> 4) - 8 * h).astype(F32) + off_r * (1.0 / PITCH)
    step_c = (lc - (lane & 15)).astype(F32) + off_c * (1.0 / PITCH)
    total = jnp.sum(e, axis=0, keepdims=True)
    t_r = jnp.sum(e * step_r, axis=0, keepdims=True) / total
    t_c = jnp.sum(e * step_c, axis=0, keepdims=True) / total
    return jnp.concatenate([t_r, t_c], axis=0)


def lower_planes(lower, p):
    return [lower[512 + 64 * p + 16 * n : 528 + 64 * p + 16 * n, :].astype(F32) for n in range(4)]


def inner_scores(patches, cand, xb, xa, lower, inner, left, right):
    row, col = tile_place()
    sort_halos(col, left, right, xa, xb)

    def sides(d):
        at = slice(d * 32, d * 32 + 32)
        return patches[d], left[at, :], right[at, :]

    def one(s, z):
        pieces = sides(s + z + 1)
        for h in range(2):
            lanes = slice(h * HALF, h * HALF + HALF)
            lr, lc = local_place(cand[s, z, :, lanes], row, col)
            inner[z, s, h] = inner_half(h, patches[s, lanes, :], *pieces, lr, lc)

    for s in range(SEC - 1):
        one(s, 0)
        if s < SEC - 2:
            one(s, 1)
    for p, (s, z) in enumerate(CROSS):
        pieces = sides(s + z + 1 - SEC)
        planes = lower_planes(lower, p)
        for h in range(2):
            mine = lower[256 * (s - 6) + HALF * h : 256 * (s - 6) + HALF * h + HALF, :]
            lr, lc = [plane[8 * h : 8 * h + 8].astype(I32) for plane in planes[:2]]
            inner[z, s + 2, h] = inner_half(h, mine, *pieces, lr, lc)


def lower_targets(start, rb, ra, cb, ca, lower, inner, sent):
    row, _ = tile_place()
    even = row % 2 == 0

    def pick(p, q, at):
        return jnp.where(even, q[at], p[at]), jnp.where(even, p[at], q[at])

    strips = [pick(ra, rb, d) for d in range(2)]
    corners = pick(ca, cb, slice(0, 16))
    for p, (s, z) in enumerate(CROSS):
        d = s + z + 1 - SEC
        mine = lower[256 * (s - 6) : 256 * (s - 6) + 256, :]
        planes = lower_planes(lower, p)
        for h in range(2):
            lanes = slice(h * HALF, h * HALF + HALF)
            lr, lc, off_r, off_c = [plane[8 * h : 8 * h + 8] for plane in planes]
            sent[2 * p : 2 * p + 2, lanes] = half_targets(
                h, mine[lanes, :], inner[z, s + 2, h], strips[d][h], (corners[h], 8 * d),
                lr.astype(I32), lc.astype(I32), off_r, off_c,
            )
    sent[6:8, :] = start[0]
    sent[8:10, :] = start[1]
    sent[10:16, :] = jnp.zeros((6, VT), F32)


def own_targets(
    patches, cand, offs, pairs, start, xb, xa, rb, ra, cb, ca, lower, inner, sent,
    p0, p1, u1, t0, t1, c0, c1, cross, low,
    left, right, above, below, top, bottom, tall,
):
    row, col = tile_place()
    stack = lax.axis_index("stack").astype(I32)
    sort_halos(col, left, right, xa, xb)
    sort_halos(row, above, below, ra, rb)
    sort_halos(row, top, bottom, ca, cb)

    def one(s, z, store, corner_first):
        d = s + z + 1

        for h in range(2):
            strip, src = (above, top) if h == 0 else (below, bottom)
            at = slice(d // 2 * 16, d // 2 * 16 + 16)
            lanes = slice(h * HALF, h * HALF + HALF)
            lr, lc = local_place(cand[s, z, :, lanes], row, col)
            store[s, :, lanes] = half_targets(
                h, patches[s, lanes, :], inner[z, s, h], strip[d], (src[at, :], corner_first), lr, lc,
                offs[s, z, 0, :, lanes].astype(F32), offs[s, z, 1, :, lanes].astype(F32),
            )

    for s in range(SEC - 1):
        one(s, 0, p0, 8 * ((s + 1) % 2))
        if s < SEC - 2:
            one(s, 1, p1, 8 * (s % 2))

    nothing = jnp.zeros((2, VT), F32)
    p0[7] = nothing
    p1[6] = nothing
    p1[7] = nothing

    tied = jnp.where(stack == 0, 0.0, lower[704:720, :].astype(F32))
    last = stack == lax.axis_size("stack") - 1
    for z, p, t, c in ((0, p0, t0, c0), (1, p1, t1, c1)):
        rows_of(p, t, 4)
        t[0:4, :] = jnp.zeros((4, VT), F32)
        c[0:4, :] = jnp.zeros((4, VT), F32)
        for s in range(SEC):
            here = jnp.full((2, VT), pairs[z, s], I32).astype(F32)
            if (s, z) in CROSS:
                n = CROSS.index((s, z))
                cross[2 * n : 2 * n + 2, :] = jnp.where(last, 0.0, here)
                here = nothing
            c[4 + 2 * s : 6 + 2 * s, :] = here
    cross[6:8, :] = nothing
    for p, (s, z) in enumerate(CROSS):
        t, c = ((t0, c0), (t1, c1))[z]
        at = 2 * (s - 6)
        t[at : at + 2, :] = sent[2 * p : 2 * p + 2, :]
        line = tied[p : p + 1, :]
        c[at : at + 2, :] = jnp.broadcast_to(jnp.concatenate([line, line], axis=1), (2, VT))
    ends = lower[720:736, :].astype(F32)
    tall[0:4, 0:HALF] = ends[0:4] + ends[8:12]
    tall[0:4, HALF:VT] = ends[4:8] + ends[12:16]
    rows_of(start, tall, 4)
    tall[20:24, :] = jnp.zeros((4, VT), F32)
    u = tall[4:20, :]

    def whole(ref):
        part = [ref[256 + 16 * n : 272 + 16 * n, :].astype(F32) for n in range(4)]
        return jnp.concatenate([part[0] + part[2], part[1] + part[3]], axis=1)

    def half(ref):
        part = ref[64:80, :].astype(F32) + ref[80:96, :].astype(F32)
        return jnp.concatenate([part, part], axis=1)

    plane = laplace(u, whole(left), whole(right), half(top), half(bottom), row, col)
    u1[...] = relaxed(u, tall, t0, t1, c0, c1, plane)
    base, own = tall[0:4, :], tall[4:8, :]
    near = jnp.concatenate([own[0:2], own[0:2]], axis=0)
    far = jnp.concatenate([jnp.zeros((2, VT), F32), own[2:4]], axis=0)
    got0 = jnp.concatenate([sent[0:2, :], sent[2:4, :]], axis=0)
    got1 = jnp.concatenate([nothing, sent[4:6, :]], axis=0)
    tied0 = jnp.concatenate([c1[0:2, :], c0[2:4, :]], axis=0)
    tied1 = jnp.concatenate([nothing, c1[2:4, :]], axis=0)
    low[0:4, :] = STEP * (tied0 * (near - base - got0) + tied1 * (far - base - got1))
    low[4:8, :] = jnp.zeros((4, VT), F32)


def sort_halos(index, first, second, p, q):
    @pl.when(index % 2 == 0)
    def _():
        first[...] = q[...]
        second[...] = p[...]

    @pl.when(index % 2 == 1)
    def _():
        first[...] = p[...]
        second[...] = q[...]


def laplace(u, left, right, above, below, row, col):
    lane = iota(u.shape, 1)
    b = lane & 15
    up = jnp.where(lane < SIDE, pltpu.roll(above, SIDE, 1), pltpu.roll(u, SIDE, 1))
    up = jnp.where((lane < SIDE) & (row == 0), u, up)
    down = jnp.where(lane >= VT - SIDE, pltpu.roll(below, VT - SIDE, 1), pltpu.roll(u, VT - SIDE, 1))
    down = jnp.where((lane >= VT - SIDE) & (row == COLS - 1), u, down)
    west = jnp.where(b == 0, pltpu.roll(left, VT - SIDE + 1, 1), pltpu.roll(u, 1, 1))
    west = jnp.where((b == 0) & (col == 0), u, west)
    east = jnp.where(b == SIDE - 1, pltpu.roll(right, SIDE - 1, 1), pltpu.roll(u, VT - 1, 1))
    east = jnp.where((b == SIDE - 1) & (col == COLS - 1), u, east)
    return ((down - u) - (u - up)) + ((east - u) - (u - west))


def relaxed(u, tall, t0, t1, c0, c1, plane):
    base = tall[0:20, :]
    s0 = c0[0:20, :] * (tall[2:22, :] - base - t0[0:20, :])
    s1 = c1[0:20, :] * (tall[4:24, :] - base - t1[0:20, :])
    zforce = s0[4:20] - s0[2:18] + s1[4:20] - s1[0:16]
    return u + STEP * (plane + zforce)


def cross_force(u, upper, got, cross):
    near, far = upper[0:2], upper[2:4]
    six = cross[0:2, :] * (near - u[12:14] - got[0:2, :])
    seven = cross[2:4, :] * (near - u[14:16] - got[2:4, :]) + cross[4:6, :] * (far - u[14:16] - got[4:6, :])
    return jnp.concatenate([jnp.zeros((12, VT), F32), six, seven], axis=0)


def first_round(start, part, got, cross, u1):
    u0 = jnp.concatenate([jnp.zeros((12, VT), F32), start[6], start[7]], axis=0)
    u1[...] = part[...] + STEP * cross_force(u0, got[6:10, :], got, cross)


def all_targets(p0, p1, got, targets):
    stack = lax.axis_index("stack").astype(I32)
    last = stack == lax.axis_size("stack") - 1
    for s in range(SEC):
        for z, p in ((0, p0), (1, p1)):
            if (s, z) in CROSS:
                n = CROSS.index((s, z))
                targets[s, z] = jnp.where(last, 0.0, got[2 * n : 2 * n + 2, :])
            else:
                targets[s, z] = p[s]


def second_round(u1, sb, sa, xa, xb, ra, rb, t0, t1, c0, c1, cross, low, got, out, tall):
    row, col = tile_place()
    stack = lax.axis_index("stack").astype(I32)
    col_even, row_even, stack_even = col % 2 == 0, row % 2 == 0, stack % 2 == 0
    u = u1[...]
    tall[4:20, :] = u
    below_rows = jnp.where(stack_even, sb[12:16, :], sa[12:16, :])
    upper = jnp.where(stack_even, sa[0:4, :], sb[0:4, :])
    tall[0:4, :] = below_rows + low[0:4, :]
    tall[20:24, :] = jnp.zeros((4, VT), F32)
    plane = laplace(
        u,
        jnp.where(col_even, xb[...], xa[...]),
        jnp.where(col_even, xa[...], xb[...]),
        jnp.where(row_even, rb[...], ra[...]),
        jnp.where(row_even, ra[...], rb[...]),
        row,
        col,
    )
    u = relaxed(u, tall, t0, t1, c0, c1, plane + cross_force(u, upper, got, cross))
    for s in range(SEC):
        out[s] = u[2 * s : 2 * s + 2]


def shape(*dims, dtype=F32):
    return jax.ShapeDtypeStruct(dims, dtype)


def call(body, outs, scratch, flops, n_in, smem=(), far=(), vmem=24 << 20):
    def space(n):
        return pltpu.SMEM if n in smem else pltpu.HBM if n in far else pltpu.VMEM

    return pl.pallas_call(
        body,
        out_shape=outs,
        in_specs=[pl.BlockSpec(memory_space=space(n)) for n in range(n_in)],
        out_specs=[pl.BlockSpec(memory_space=pltpu.VMEM) for _ in outs],
        scratch_shapes=scratch,
        name=body.__name__,
        compiler_params=pltpu.CompilerParams(vmem_limit_bytes=vmem),
        cost_estimate=pl.CostEstimate(flops=flops, bytes_accessed=1 << 20, transcendentals=0),
    )


def on_device(patches, cand, offs, pairs, start):
    pairs = pairs.T
    flat = pltpu.VMEM((16, VT), F32)
    held = [
        pltpu.VMEM((SEC, VT, PATCH), BF),
        pltpu.VMEM((2, 2, 8, VT), I32),
        pltpu.VMEM((2, 2, 2, 8, VT), I32),
        pltpu.VMEM((2, SEC), I32),
        pltpu.VMEM((SEC, 2, VT), F32),
        pltpu.SemaphoreType.DMA((4 + SEC,)),
    ]
    outs = [shape(SEC, 32, PATCH, dtype=BF)] * 2 + [shape(X_ROWS, PATCH, dtype=BF)] * 2 + [shape(S_ROWS, PATCH, dtype=BF)]
    outs = [pltpu.VMEM(a.shape, a.dtype) for a in outs]
    rb, ra, xb, xa, lower = call(pack_first, outs, [flat] + held, 1 << 20, 5, far=(0, 1, 2, 3, 4), vmem=58 << 20)(
        patches, cand, offs, pairs, start
    )
    rb = swapped(rb, "tile", row_b)
    ra = swapped(ra, "tile", row_a)
    xa = swapped(xa, "tile", col_a)
    xb = swapped(xb, "tile", col_b)
    lower = swapped(lower, "stack", lambda i: (i + 1) % 16)
    cb, ca = call(pack_corners, [shape(C_ROWS, PATCH, dtype=BF)] * 2, [flat], 1 << 20, 3)(start, xb, xa)
    cb = swapped(cb, "tile", row_b)
    ca = swapped(ca, "tile", row_a)
    halos = (xb, xa, rb, ra, cb, ca)
    (inner,) = call(
        inner_scores, [shape(2, SEC + 2, 2, 8, HALF)], [pltpu.VMEM((X_ROWS, PATCH), BF)] * 2, 1 << 31, 5
    )(patches, cand, xb, xa, lower)
    (sent,) = call(lower_targets, [shape(16, VT)], [], 1 << 20, 7)(start, rb, ra, cb, ca, lower, inner)
    got = swapped(sent, "stack", lambda i: (i - 1) % 16)
    p0, p1, part, t0, t1, c0, c1, cross, low = call(
        own_targets,
        [shape(SEC, 2, VT)] * 2 + [shape(16, VT)] + [shape(24, VT)] * 4 + [shape(8, VT)] * 2,
        [pltpu.VMEM(a.shape, BF) for a in halos] + [pltpu.VMEM((24, VT), F32)],
        1 << 31,
        14,
        smem=(3,),
    )(patches, cand, offs, pairs, start, *halos, lower, inner, sent)
    sa = swapped(part, "stack", stack_a)
    sb = swapped(part, "stack", stack_b)
    (u1,) = call(first_round, [shape(16, VT)], [], 1 << 16, 4)(start, part, got, cross)
    moved = [swapped(u1, "tile", partner) for partner in (col_a, col_b, row_a, row_b)]
    (targets,) = call(all_targets, [shape(SEC, 2, 2, VT)], [], 1 << 20, 3)(p0, p1, got)
    (aligned,) = call(second_round, [shape(SEC, 2, VT)], [pltpu.VMEM((24, VT), F32)], 1 << 20, 14)(
        u1, sb, sa, *moved, t0, t1, c0, c1, cross, low, got
    )
    return aligned, targets


def solution(mesh):
    placed = (
        P("stack", "tile", None),
        P("stack", None, None, "tile"),
        P("stack", None, None, None, "tile"),
        P("stack", None),
        P("stack", None, "tile"),
    )
    return jax.shard_map(
        on_device,
        mesh=mesh,
        in_specs=placed,
        out_specs=(P("stack", None, "tile"), P("stack", None, None, "tile")),
        check_vma=False,
    )
```

```python
import jax
import jax.numpy as jnp
from jax import lax
from jax.experimental import pallas as pl
from jax.experimental.pallas import tpu as pltpu
from jax.sharding import PartitionSpec as P

SIDE = 16
COLS = 4
PATCH = 128
VT = 256
HALF = 128
SEC = 8
PITCH = 128.0
STEP = 0.1
BF = jnp.bfloat16
F32 = jnp.float32
I32 = jnp.int32

X_ROWS = 8 * 32 + 64
C_ROWS = 64 + 32
S_ROWS = 736
CROSS = ((6, 1), (7, 0), (7, 1))


def swapped(block, axis, partner):
    return lax.ppermute(block, axis, [(i, partner(i)) for i in range(lax.axis_size(axis))])


def col_a(i):
    return i ^ 1


def col_b(i):
    return i // COLS * COLS + (COLS - 1 - i % COLS)


def row_a(i):
    return i ^ COLS


def row_b(i):
    return (COLS - 1 - i // COLS) * COLS + i % COLS


def stack_a(i):
    return i ^ 1


def stack_b(i):
    return (((i + 1) ^ 1) - 1) % 16


def tile_place():
    tile = lax.axis_index("tile").astype(I32)
    return tile // COLS, tile % COLS


def iota(shape, dim):
    return lax.broadcasted_iota(I32, shape, dim)


def two_parts(u):
    hi = u.astype(BF)
    return hi, (u - hi.astype(F32)).astype(BF)


def rows_of(start_ref, scr, first=0):
    for s in range(SEC):
        scr[first + 2 * s : first + 2 * s + 2, :] = start_ref[s]


def dot(a, b):
    return lax.dot_general(a, b, (((1,), (0,)), ((), ())), preferred_element_type=F32)


def dot_t(a, b):
    return lax.dot_general(a, b, (((1,), (1,)), ((), ())), preferred_element_type=F32)


def pack_first(
    patches, cand, offs, pairs, start, rb, ra, xb, xa, lower,
    scr, held, held_c, held_o, held_p, held_u, sems,
):
    sources = [(start, held_u), (pairs, held_p), (cand.at[6:8], held_c), (offs.at[6:8], held_o)]
    sources += [(patches.at[s : s + 4], held.at[s : s + 4]) for s in range(0, SEC, 4)]
    copies = [pltpu.make_async_copy(src, dst, sems.at[n]) for n, (src, dst) in enumerate(sources)]
    for copy in copies:
        copy.start()
    row, col = tile_place()
    off_a = jnp.where(col % 2 == 0, SIDE - 2, 0)
    j = iota((64, VT), 0)
    v = iota((64, VT), 1)
    off = jnp.where(j < 32, off_a, SIDE - 2 - off_a)
    source = (j % SIDE) * SIDE + off + (j % 32) // SIDE
    pick = (v == source).astype(BF)
    for copy in copies[:4]:
        copy.wait()
    rows_of(held_u, scr)
    hi, lo = two_parts(scr[...])
    for n, part in enumerate((hi[:, :HALF], hi[:, HALF:], lo[:, :HALF], lo[:, HALF:])):
        xa[256 + 16 * n : 272 + 16 * n, :] = part
        xb[256 + 16 * n : 272 + 16 * n, :] = part
    r = iota((16, HALF), 0)
    tied = jnp.zeros((16, HALF), F32)
    for p, (s, z) in enumerate(CROSS):
        lr, lc = local_place(held_c[s - 6, z], row, col)
        for n, plane in enumerate((lr, lc, held_o[s - 6, z, 0], held_o[s - 6, z, 1])):
            at = 512 + 64 * p + 16 * n
            plane = plane.astype(F32)
            lower[at : at + 16, :] = jnp.concatenate([plane[:, :HALF], plane[:, HALF:]], axis=0).astype(BF)
        tied = jnp.where(r == p, held_p[z : z + 1, s : s + 1].astype(F32), tied)
    lower[704:720, :] = tied.astype(BF)
    h, low = two_parts(scr[12:16, :])
    h, low = h.astype(F32), low.astype(F32)
    lower[720:736, :] = jnp.concatenate(
        [h[:, :HALF], h[:, HALF:], low[:, :HALF], low[:, HALF:]], axis=0
    ).astype(BF)
    first = jnp.where(row % 2 == 0, VT - 32, 0)
    for s in range(SEC):
        if s % 4 == 0:
            copies[4 + s // 4].wait()
        strips = dot(pick, held[s]).astype(BF)
        xa[s * 32 : s * 32 + 32, :] = strips[:32]
        xb[s * 32 : s * 32 + 32, :] = strips[32:]
        ra[s] = held[s, pl.ds(pl.multiple_of(first, 32), 32), :]
        rb[s] = held[s, pl.ds(pl.multiple_of(VT - 32 - first, 32), 32), :]
        if s >= 6:
            lower[(s - 6) * 256 : (s - 5) * 256, :] = held[s]


def pack_corners(start, xb, xa, cb, ca, scr):
    row, col = tile_place()
    off_a = jnp.where(row % 2 == 0, SIDE - 2, 0)
    both = jnp.concatenate([xa[0:256, :], xb[0:256, :]], axis=0)
    q = iota((128, 512), 0)
    k = iota((128, 512), 1)
    off = jnp.where(q < 64, off_a, SIDE - 2 - off_a)
    side = (q % 8) // 4
    buffer = jnp.where(col % 2 == 0, 1 - side, side)
    source = buffer * 256 + (q % 64) // 8 * 32 + (q % 4) // 2 * SIDE + off + q % 2
    corners = dot((k == source).astype(BF), both).astype(BF)
    ca[0:64, :] = corners[:64]
    cb[0:64, :] = corners[64:]
    rows_of(start, scr)
    hi, lo = two_parts(scr[...])
    even = row % 2 == 0
    for out, second in ((ca, even), (cb, jnp.logical_not(even))):

        @pl.when(second)
        def _():
            out[64:80, :] = hi[:, HALF:]
            out[80:96, :] = lo[:, HALF:]

        @pl.when(jnp.logical_not(second))
        def _():
            out[64:80, :] = hi[:, :HALF]
            out[80:96, :] = lo[:, :HALF]


def local_place(ids, row, col):
    tile = ids >> 8
    lr = (tile >> 2) * SIDE + ((ids >> 4) & 15) - row * SIDE
    lc = (tile & 3) * SIDE + (ids & 15) - col * SIDE
    return lr, lc


def picked(scores, slot, sub, vregs, score):
    for n, at in enumerate(vregs):
        got = jnp.take_along_axis(scores[at : at + 8], sub, axis=0)
        score = jnp.where(slot == n, got, score)
    return score


def inner_half(h, mine, own, left, right, lr, lc):
    table = jnp.concatenate([own[0:160] if h == 0 else own[96:256], left, right], axis=0)
    scores = dot_t(table, mine)
    i = lr if h == 0 else lr - 6
    outside_c = (lc < 0) | (lc >= SIDE)
    side = jnp.where(lc >= SIDE, 1, 0)
    slot = jnp.where(outside_c, 20 + side * 4 + (lc & 1) * 2 + (lr >> 3), i * 2 + (lc >> 3))
    slot = jnp.where((lr < 0) | (lr >= SIDE), -1, slot)
    sub = jnp.where(outside_c, lr & 7, lc & 7)
    return picked(scores, slot, sub, range(0, 224, 8), jnp.zeros((8, HALF), F32))


def half_targets(h, mine, score, strip, corner, lr, lc, off_r, off_c):
    rows, first = corner
    scores = dot_t(jnp.concatenate([strip, rows], axis=0), mine)
    outside_c = (lc < 0) | (lc >= SIDE)
    side = jnp.where(lc >= SIDE, 1, 0)
    beyond = lr < 0 if h == 0 else lr >= SIDE
    slot = jnp.where(outside_c, 4, (lr & 1) * 2 + (lc >> 3))
    slot = jnp.where(beyond, slot, -1)
    sub = jnp.where(outside_c, side * 4 + (lc & 1) * 2 + (lr & 1), lc & 7)
    score = picked(scores, slot, sub, (0, 8, 16, 24, 32 + first), score)
    score = score * PATCH ** (-0.5)
    e = jnp.exp(score - jnp.max(score, axis=0, keepdims=True))
    lane = iota((8, HALF), 1)
    step_r = (lr - (lane >> 4) - 8 * h).astype(F32) + off_r * (1.0 / PITCH)
    step_c = (lc - (lane & 15)).astype(F32) + off_c * (1.0 / PITCH)
    total = jnp.sum(e, axis=0, keepdims=True)
    t_r = jnp.sum(e * step_r, axis=0, keepdims=True) / total
    t_c = jnp.sum(e * step_c, axis=0, keepdims=True) / total
    return jnp.concatenate([t_r, t_c], axis=0)


def lower_planes(lower, p):
    return [lower[512 + 64 * p + 16 * n : 528 + 64 * p + 16 * n, :].astype(F32) for n in range(4)]


def inner_scores(patches, cand, xb, xa, lower, inner, left, right):
    row, col = tile_place()
    sort_halos(col, left, right, xa, xb)

    def sides(d):
        at = slice(d * 32, d * 32 + 32)
        return patches[d], left[at, :], right[at, :]

    def one(s, z):
        pieces = sides(s + z + 1)
        for h in range(2):
            lanes = slice(h * HALF, h * HALF + HALF)
            lr, lc = local_place(cand[s, z, :, lanes], row, col)
            inner[z, s, h] = inner_half(h, patches[s, lanes, :], *pieces, lr, lc)

    for s in range(SEC - 1):
        one(s, 0)
        if s < SEC - 2:
            one(s, 1)
    for p, (s, z) in enumerate(CROSS):
        pieces = sides(s + z + 1 - SEC)
        planes = lower_planes(lower, p)
        for h in range(2):
            mine = lower[256 * (s - 6) + HALF * h : 256 * (s - 6) + HALF * h + HALF, :]
            lr, lc = [plane[8 * h : 8 * h + 8].astype(I32) for plane in planes[:2]]
            inner[z, s + 2, h] = inner_half(h, mine, *pieces, lr, lc)


def lower_targets(start, rb, ra, cb, ca, lower, inner, sent):
    row, _ = tile_place()
    even = row % 2 == 0

    def pick(p, q, at):
        return jnp.where(even, q[at], p[at]), jnp.where(even, p[at], q[at])

    strips = [pick(ra, rb, d) for d in range(2)]
    corners = pick(ca, cb, slice(0, 16))
    for p, (s, z) in enumerate(CROSS):
        d = s + z + 1 - SEC
        mine = lower[256 * (s - 6) : 256 * (s - 6) + 256, :]
        planes = lower_planes(lower, p)
        for h in range(2):
            lanes = slice(h * HALF, h * HALF + HALF)
            lr, lc, off_r, off_c = [plane[8 * h : 8 * h + 8] for plane in planes]
            sent[2 * p : 2 * p + 2, lanes] = half_targets(
                h, mine[lanes, :], inner[z, s + 2, h], strips[d][h], (corners[h], 8 * d),
                lr.astype(I32), lc.astype(I32), off_r, off_c,
            )
    sent[6:8, :] = start[0]
    sent[8:10, :] = start[1]
    sent[10:16, :] = jnp.zeros((6, VT), F32)


def own_targets(
    patches, cand, offs, pairs, start, xb, xa, rb, ra, cb, ca, lower, inner, sent,
    p0, p1, u1, t0, t1, c0, c1, cross, low,
    left, right, above, below, top, bottom, tall,
):
    row, col = tile_place()
    stack = lax.axis_index("stack").astype(I32)
    sort_halos(col, left, right, xa, xb)
    sort_halos(row, above, below, ra, rb)
    sort_halos(row, top, bottom, ca, cb)

    def one(s, z, store, corner_first):
        d = s + z + 1

        for h in range(2):
            strip, src = (above, top) if h == 0 else (below, bottom)
            at = slice(d // 2 * 16, d // 2 * 16 + 16)
            lanes = slice(h * HALF, h * HALF + HALF)
            lr, lc = local_place(cand[s, z, :, lanes], row, col)
            store[s, :, lanes] = half_targets(
                h, patches[s, lanes, :], inner[z, s, h], strip[d], (src[at, :], corner_first), lr, lc,
                offs[s, z, 0, :, lanes].astype(F32), offs[s, z, 1, :, lanes].astype(F32),
            )

    for s in range(SEC - 1):
        one(s, 0, p0, 8 * ((s + 1) % 2))
        if s < SEC - 2:
            one(s, 1, p1, 8 * (s % 2))

    nothing = jnp.zeros((2, VT), F32)
    p0[7] = nothing
    p1[6] = nothing
    p1[7] = nothing

    tied = jnp.where(stack == 0, 0.0, lower[704:720, :].astype(F32))
    last = stack == lax.axis_size("stack") - 1
    for z, p, t, c in ((0, p0, t0, c0), (1, p1, t1, c1)):
        rows_of(p, t, 4)
        t[0:4, :] = jnp.zeros((4, VT), F32)
        c[0:4, :] = jnp.zeros((4, VT), F32)
        for s in range(SEC):
            here = jnp.full((2, VT), pairs[z, s], I32).astype(F32)
            if (s, z) in CROSS:
                n = CROSS.index((s, z))
                cross[2 * n : 2 * n + 2, :] = jnp.where(last, 0.0, here)
                here = nothing
            c[4 + 2 * s : 6 + 2 * s, :] = here
    cross[6:8, :] = nothing
    for p, (s, z) in enumerate(CROSS):
        t, c = ((t0, c0), (t1, c1))[z]
        at = 2 * (s - 6)
        t[at : at + 2, :] = sent[2 * p : 2 * p + 2, :]
        line = tied[p : p + 1, :]
        c[at : at + 2, :] = jnp.broadcast_to(jnp.concatenate([line, line], axis=1), (2, VT))
    ends = lower[720:736, :].astype(F32)
    tall[0:4, 0:HALF] = ends[0:4] + ends[8:12]
    tall[0:4, HALF:VT] = ends[4:8] + ends[12:16]
    rows_of(start, tall, 4)
    tall[20:24, :] = jnp.zeros((4, VT), F32)
    u = tall[4:20, :]

    def whole(ref):
        part = [ref[256 + 16 * n : 272 + 16 * n, :].astype(F32) for n in range(4)]
        return jnp.concatenate([part[0] + part[2], part[1] + part[3]], axis=1)

    def half(ref):
        part = ref[64:80, :].astype(F32) + ref[80:96, :].astype(F32)
        return jnp.concatenate([part, part], axis=1)

    plane = laplace(u, whole(left), whole(right), half(top), half(bottom), row, col)
    u1[...] = relaxed(u, tall, t0, t1, c0, c1, plane)
    base, own = tall[0:4, :], tall[4:8, :]
    near = jnp.concatenate([own[0:2], own[0:2]], axis=0)
    far = jnp.concatenate([jnp.zeros((2, VT), F32), own[2:4]], axis=0)
    got0 = jnp.concatenate([sent[0:2, :], sent[2:4, :]], axis=0)
    got1 = jnp.concatenate([nothing, sent[4:6, :]], axis=0)
    tied0 = jnp.concatenate([c1[0:2, :], c0[2:4, :]], axis=0)
    tied1 = jnp.concatenate([nothing, c1[2:4, :]], axis=0)
    low[0:4, :] = STEP * (tied0 * (near - base - got0) + tied1 * (far - base - got1))
    low[4:8, :] = jnp.zeros((4, VT), F32)


def sort_halos(index, first, second, p, q):
    @pl.when(index % 2 == 0)
    def _():
        first[...] = q[...]
        second[...] = p[...]

    @pl.when(index % 2 == 1)
    def _():
        first[...] = p[...]
        second[...] = q[...]


def laplace(u, left, right, above, below, row, col):
    lane = iota(u.shape, 1)
    b = lane & 15
    up = jnp.where(lane < SIDE, pltpu.roll(above, SIDE, 1), pltpu.roll(u, SIDE, 1))
    up = jnp.where((lane < SIDE) & (row == 0), u, up)
    down = jnp.where(lane >= VT - SIDE, pltpu.roll(below, VT - SIDE, 1), pltpu.roll(u, VT - SIDE, 1))
    down = jnp.where((lane >= VT - SIDE) & (row == COLS - 1), u, down)
    west = jnp.where(b == 0, pltpu.roll(left, VT - SIDE + 1, 1), pltpu.roll(u, 1, 1))
    west = jnp.where((b == 0) & (col == 0), u, west)
    east = jnp.where(b == SIDE - 1, pltpu.roll(right, SIDE - 1, 1), pltpu.roll(u, VT - 1, 1))
    east = jnp.where((b == SIDE - 1) & (col == COLS - 1), u, east)
    return ((down - u) - (u - up)) + ((east - u) - (u - west))


def relaxed(u, tall, t0, t1, c0, c1, plane):
    base = tall[0:20, :]
    s0 = c0[0:20, :] * (tall[2:22, :] - base - t0[0:20, :])
    s1 = c1[0:20, :] * (tall[4:24, :] - base - t1[0:20, :])
    zforce = s0[4:20] - s0[2:18] + s1[4:20] - s1[0:16]
    return u + STEP * (plane + zforce)


def cross_force(u, upper, got, cross):
    near, far = upper[0:2], upper[2:4]
    six = cross[0:2, :] * (near - u[12:14] - got[0:2, :])
    seven = cross[2:4, :] * (near - u[14:16] - got[2:4, :]) + cross[4:6, :] * (far - u[14:16] - got[4:6, :])
    return jnp.concatenate([jnp.zeros((12, VT), F32), six, seven], axis=0)


def first_round(start, part, got, cross, u1):
    u0 = jnp.concatenate([jnp.zeros((12, VT), F32), start[6], start[7]], axis=0)
    u1[...] = part[...] + STEP * cross_force(u0, got[6:10, :], got, cross)


def all_targets(p0, p1, got, targets):
    stack = lax.axis_index("stack").astype(I32)
    last = stack == lax.axis_size("stack") - 1
    for s in range(SEC):
        for z, p in ((0, p0), (1, p1)):
            if (s, z) in CROSS:
                n = CROSS.index((s, z))
                targets[s, z] = jnp.where(last, 0.0, got[2 * n : 2 * n + 2, :])
            else:
                targets[s, z] = p[s]


def second_round(u1, sb, sa, xa, xb, ra, rb, t0, t1, c0, c1, cross, low, got, out, tall):
    row, col = tile_place()
    stack = lax.axis_index("stack").astype(I32)
    col_even, row_even, stack_even = col % 2 == 0, row % 2 == 0, stack % 2 == 0
    u = u1[...]
    tall[4:20, :] = u
    below_rows = jnp.where(stack_even, sb[12:16, :], sa[12:16, :])
    upper = jnp.where(stack_even, sa[0:4, :], sb[0:4, :])
    tall[0:4, :] = below_rows + low[0:4, :]
    tall[20:24, :] = jnp.zeros((4, VT), F32)
    plane = laplace(
        u,
        jnp.where(col_even, xb[...], xa[...]),
        jnp.where(col_even, xa[...], xb[...]),
        jnp.where(row_even, rb[...], ra[...]),
        jnp.where(row_even, ra[...], rb[...]),
        row,
        col,
    )
    u = relaxed(u, tall, t0, t1, c0, c1, plane + cross_force(u, upper, got, cross))
    for s in range(SEC):
        out[s] = u[2 * s : 2 * s + 2]


def shape(*dims, dtype=F32):
    return jax.ShapeDtypeStruct(dims, dtype)


def call(body, outs, scratch, flops, n_in, smem=(), far=(), vmem=24 << 20):
    def space(n):
        return pltpu.SMEM if n in smem else pltpu.HBM if n in far else pltpu.VMEM

    return pl.pallas_call(
        body,
        out_shape=outs,
        in_specs=[pl.BlockSpec(memory_space=space(n)) for n in range(n_in)],
        out_specs=[pl.BlockSpec(memory_space=pltpu.VMEM) for _ in outs],
        scratch_shapes=scratch,
        name=body.__name__,
        compiler_params=pltpu.CompilerParams(vmem_limit_bytes=vmem),
        cost_estimate=pl.CostEstimate(flops=flops, bytes_accessed=1 << 20, transcendentals=0),
    )


def on_device(patches, cand, offs, pairs, start):
    pairs = pairs.T
    flat = pltpu.VMEM((16, VT), F32)
    held = [
        pltpu.VMEM((SEC, VT, PATCH), BF),
        pltpu.VMEM((2, 2, 8, VT), I32),
        pltpu.VMEM((2, 2, 2, 8, VT), I32),
        pltpu.VMEM((2, SEC), I32),
        pltpu.VMEM((SEC, 2, VT), F32),
        pltpu.SemaphoreType.DMA((4 + SEC,)),
    ]
    outs = [shape(SEC, 32, PATCH, dtype=BF)] * 2 + [shape(X_ROWS, PATCH, dtype=BF)] * 2 + [shape(S_ROWS, PATCH, dtype=BF)]
    outs = [pltpu.VMEM(a.shape, a.dtype) for a in outs]
    rb, ra, xb, xa, lower = call(pack_first, outs, [flat] + held, 1 << 20, 5, far=(0, 1, 2, 3, 4), vmem=58 << 20)(
        patches, cand, offs, pairs, start
    )
    rb = swapped(rb, "tile", row_b)
    ra = swapped(ra, "tile", row_a)
    xa = swapped(xa, "tile", col_a)
    xb = swapped(xb, "tile", col_b)
    lower = swapped(lower, "stack", lambda i: (i + 1) % 16)
    cb, ca = call(pack_corners, [shape(C_ROWS, PATCH, dtype=BF)] * 2, [flat], 1 << 20, 3)(start, xb, xa)
    cb = swapped(cb, "tile", row_b)
    ca = swapped(ca, "tile", row_a)
    halos = (xb, xa, rb, ra, cb, ca)
    (inner,) = call(
        inner_scores, [shape(2, SEC + 2, 2, 8, HALF)], [pltpu.VMEM((X_ROWS, PATCH), BF)] * 2, 1 << 31, 5
    )(patches, cand, xb, xa, lower)
    (sent,) = call(lower_targets, [shape(16, VT)], [], 1 << 20, 7)(start, rb, ra, cb, ca, lower, inner)
    got = swapped(sent, "stack", lambda i: (i - 1) % 16)
    p0, p1, part, t0, t1, c0, c1, cross, low = call(
        own_targets,
        [shape(SEC, 2, VT)] * 2 + [shape(16, VT)] + [shape(24, VT)] * 4 + [shape(8, VT)] * 2,
        [pltpu.VMEM(a.shape, BF) for a in halos] + [pltpu.VMEM((24, VT), F32)],
        1 << 31,
        14,
        smem=(3,),
    )(patches, cand, offs, pairs, start, *halos, lower, inner, sent)
    sa = swapped(part, "stack", stack_a)
    sb = swapped(part, "stack", stack_b)
    (u1,) = call(first_round, [shape(16, VT)], [], 1 << 16, 4)(start, part, got, cross)
    moved = [swapped(u1, "tile", partner) for partner in (col_a, col_b, row_a, row_b)]
    (targets,) = call(all_targets, [shape(SEC, 2, 2, VT)], [], 1 << 20, 3)(p0, p1, got)
    (aligned,) = call(second_round, [shape(SEC, 2, VT)], [pltpu.VMEM((24, VT), F32)], 1 << 20, 14)(
        u1, sb, sa, *moved, t0, t1, c0, c1, cross, low, got
    )
    return aligned, targets


def solution(mesh):
    placed = (
        P("stack", "tile", None),
        P("stack", None, None, "tile"),
        P("stack", None, None, None, "tile"),
        P("stack", None),
        P("stack", None, "tile"),
    )
    return jax.shard_map(
        on_device,
        mesh=mesh,
        in_specs=placed,
        out_specs=(P("stack", None, "tile"), P("stack", None, None, "tile")),
        check_vma=False,
    )
```

```python
import jax
import jax.numpy as jnp
from jax import lax
from jax.experimental import pallas as pl
from jax.experimental.pallas import tpu as pltpu
from jax.sharding import PartitionSpec as P

SIDE = 16
COLS = 4
PATCH = 128
VT = 256
HALF = 128
SEC = 8
PITCH = 128.0
STEP = 0.1
BF = jnp.bfloat16
F32 = jnp.float32
I32 = jnp.int32

X_ROWS = 8 * 32 + 64
C_ROWS = 64 + 32
S_ROWS = 736
CROSS = ((6, 1), (7, 0), (7, 1))


def swapped(block, axis, partner):
    return lax.ppermute(block, axis, [(i, partner(i)) for i in range(lax.axis_size(axis))])


def col_a(i):
    return i ^ 1


def col_b(i):
    return i // COLS * COLS + (COLS - 1 - i % COLS)


def row_a(i):
    return i ^ COLS


def row_b(i):
    return (COLS - 1 - i // COLS) * COLS + i % COLS


def stack_a(i):
    return i ^ 1


def stack_b(i):
    return (((i + 1) ^ 1) - 1) % 16


def tile_place():
    tile = lax.axis_index("tile").astype(I32)
    return tile // COLS, tile % COLS


def iota(shape, dim):
    return lax.broadcasted_iota(I32, shape, dim)


def two_parts(u):
    hi = u.astype(BF)
    return hi, (u - hi.astype(F32)).astype(BF)


def rows_of(start_ref, scr, first=0):
    for s in range(SEC):
        scr[first + 2 * s : first + 2 * s + 2, :] = start_ref[s]


def dot(a, b):
    return lax.dot_general(a, b, (((1,), (0,)), ((), ())), preferred_element_type=F32)


def dot_t(a, b):
    return lax.dot_general(a, b, (((1,), (1,)), ((), ())), preferred_element_type=F32)


def pack_first(
    patches, cand, offs, pairs, start, rb, ra, xb, xa, lower,
    scr, held, held_c, held_o, held_p, held_u, sems,
):
    sources = [(start, held_u), (pairs, held_p), (cand.at[6:8], held_c), (offs.at[6:8], held_o)]
    sources += [(patches.at[s : s + 8], held.at[s : s + 8]) for s in range(0, SEC, 8)]
    copies = [pltpu.make_async_copy(src, dst, sems.at[n]) for n, (src, dst) in enumerate(sources)]
    for copy in copies:
        copy.start()
    row, col = tile_place()
    off_a = jnp.where(col % 2 == 0, SIDE - 2, 0)
    j = iota((64, VT), 0)
    v = iota((64, VT), 1)
    off = jnp.where(j < 32, off_a, SIDE - 2 - off_a)
    source = (j % SIDE) * SIDE + off + (j % 32) // SIDE
    pick = (v == source).astype(BF)
    for copy in copies[:4]:
        copy.wait()
    rows_of(held_u, scr)
    hi, lo = two_parts(scr[...])
    for n, part in enumerate((hi[:, :HALF], hi[:, HALF:], lo[:, :HALF], lo[:, HALF:])):
        xa[256 + 16 * n : 272 + 16 * n, :] = part
        xb[256 + 16 * n : 272 + 16 * n, :] = part
    r = iota((16, HALF), 0)
    tied = jnp.zeros((16, HALF), F32)
    for p, (s, z) in enumerate(CROSS):
        lr, lc = local_place(held_c[s - 6, z], row, col)
        for n, plane in enumerate((lr, lc, held_o[s - 6, z, 0], held_o[s - 6, z, 1])):
            at = 512 + 64 * p + 16 * n
            plane = plane.astype(F32)
            lower[at : at + 16, :] = jnp.concatenate([plane[:, :HALF], plane[:, HALF:]], axis=0).astype(BF)
        tied = jnp.where(r == p, held_p[z : z + 1, s : s + 1].astype(F32), tied)
    lower[704:720, :] = tied.astype(BF)
    h, low = two_parts(scr[12:16, :])
    h, low = h.astype(F32), low.astype(F32)
    lower[720:736, :] = jnp.concatenate(
        [h[:, :HALF], h[:, HALF:], low[:, :HALF], low[:, HALF:]], axis=0
    ).astype(BF)
    first = jnp.where(row % 2 == 0, VT - 32, 0)
    for s in range(SEC):
        if s % 8 == 0:
            copies[4 + s // 8].wait()
        strips = dot(pick, held[s]).astype(BF)
        xa[s * 32 : s * 32 + 32, :] = strips[:32]
        xb[s * 32 : s * 32 + 32, :] = strips[32:]
        ra[s] = held[s, pl.ds(pl.multiple_of(first, 32), 32), :]
        rb[s] = held[s, pl.ds(pl.multiple_of(VT - 32 - first, 32), 32), :]
        if s >= 6:
            lower[(s - 6) * 256 : (s - 5) * 256, :] = held[s]


def pack_corners(start, xb, xa, cb, ca, scr):
    row, col = tile_place()
    off_a = jnp.where(row % 2 == 0, SIDE - 2, 0)
    both = jnp.concatenate([xa[0:256, :], xb[0:256, :]], axis=0)
    q = iota((128, 512), 0)
    k = iota((128, 512), 1)
    off = jnp.where(q < 64, off_a, SIDE - 2 - off_a)
    side = (q % 8) // 4
    buffer = jnp.where(col % 2 == 0, 1 - side, side)
    source = buffer * 256 + (q % 64) // 8 * 32 + (q % 4) // 2 * SIDE + off + q % 2
    corners = dot((k == source).astype(BF), both).astype(BF)
    ca[0:64, :] = corners[:64]
    cb[0:64, :] = corners[64:]
    rows_of(start, scr)
    hi, lo = two_parts(scr[...])
    even = row % 2 == 0
    for out, second in ((ca, even), (cb, jnp.logical_not(even))):

        @pl.when(second)
        def _():
            out[64:80, :] = hi[:, HALF:]
            out[80:96, :] = lo[:, HALF:]

        @pl.when(jnp.logical_not(second))
        def _():
            out[64:80, :] = hi[:, :HALF]
            out[80:96, :] = lo[:, :HALF]


def local_place(ids, row, col):
    tile = ids >> 8
    lr = (tile >> 2) * SIDE + ((ids >> 4) & 15) - row * SIDE
    lc = (tile & 3) * SIDE + (ids & 15) - col * SIDE
    return lr, lc


def picked(scores, slot, sub, vregs, score):
    for n, at in enumerate(vregs):
        got = jnp.take_along_axis(scores[at : at + 8], sub, axis=0)
        score = jnp.where(slot == n, got, score)
    return score


def inner_half(h, mine, own, left, right, lr, lc):
    table = jnp.concatenate([own[0:160] if h == 0 else own[96:256], left, right], axis=0)
    scores = dot_t(table, mine)
    i = lr if h == 0 else lr - 6
    outside_c = (lc < 0) | (lc >= SIDE)
    side = jnp.where(lc >= SIDE, 1, 0)
    slot = jnp.where(outside_c, 20 + side * 4 + (lc & 1) * 2 + (lr >> 3), i * 2 + (lc >> 3))
    slot = jnp.where((lr < 0) | (lr >= SIDE), -1, slot)
    sub = jnp.where(outside_c, lr & 7, lc & 7)
    return picked(scores, slot, sub, range(0, 224, 8), jnp.zeros((8, HALF), F32))


def half_targets(h, mine, score, strip, corner, lr, lc, off_r, off_c):
    rows, first = corner
    scores = dot_t(jnp.concatenate([strip, rows], axis=0), mine)
    outside_c = (lc < 0) | (lc >= SIDE)
    side = jnp.where(lc >= SIDE, 1, 0)
    beyond = lr < 0 if h == 0 else lr >= SIDE
    slot = jnp.where(outside_c, 4, (lr & 1) * 2 + (lc >> 3))
    slot = jnp.where(beyond, slot, -1)
    sub = jnp.where(outside_c, side * 4 + (lc & 1) * 2 + (lr & 1), lc & 7)
    score = picked(scores, slot, sub, (0, 8, 16, 24, 32 + first), score)
    score = score * PATCH ** (-0.5)
    e = jnp.exp(score - jnp.max(score, axis=0, keepdims=True))
    lane = iota((8, HALF), 1)
    step_r = (lr - (lane >> 4) - 8 * h).astype(F32) + off_r * (1.0 / PITCH)
    step_c = (lc - (lane & 15)).astype(F32) + off_c * (1.0 / PITCH)
    total = jnp.sum(e, axis=0, keepdims=True)
    t_r = jnp.sum(e * step_r, axis=0, keepdims=True) / total
    t_c = jnp.sum(e * step_c, axis=0, keepdims=True) / total
    return jnp.concatenate([t_r, t_c], axis=0)


def lower_planes(lower, p):
    return [lower[512 + 64 * p + 16 * n : 528 + 64 * p + 16 * n, :].astype(F32) for n in range(4)]


def inner_scores(patches, cand, xb, xa, lower, inner, left, right):
    row, col = tile_place()
    sort_halos(col, left, right, xa, xb)

    def sides(d):
        at = slice(d * 32, d * 32 + 32)
        return patches[d], left[at, :], right[at, :]

    def one(s, z):
        pieces = sides(s + z + 1)
        for h in range(2):
            lanes = slice(h * HALF, h * HALF + HALF)
            lr, lc = local_place(cand[s, z, :, lanes], row, col)
            inner[z, s, h] = inner_half(h, patches[s, lanes, :], *pieces, lr, lc)

    for s in range(SEC - 1):
        one(s, 0)
        if s < SEC - 2:
            one(s, 1)
    for p, (s, z) in enumerate(CROSS):
        pieces = sides(s + z + 1 - SEC)
        planes = lower_planes(lower, p)
        for h in range(2):
            mine = lower[256 * (s - 6) + HALF * h : 256 * (s - 6) + HALF * h + HALF, :]
            lr, lc = [plane[8 * h : 8 * h + 8].astype(I32) for plane in planes[:2]]
            inner[z, s + 2, h] = inner_half(h, mine, *pieces, lr, lc)


def lower_targets(start, rb, ra, cb, ca, lower, inner, sent):
    row, _ = tile_place()
    even = row % 2 == 0

    def pick(p, q, at):
        return jnp.where(even, q[at], p[at]), jnp.where(even, p[at], q[at])

    strips = [pick(ra, rb, d) for d in range(2)]
    corners = pick(ca, cb, slice(0, 16))
    for p, (s, z) in enumerate(CROSS):
        d = s + z + 1 - SEC
        mine = lower[256 * (s - 6) : 256 * (s - 6) + 256, :]
        planes = lower_planes(lower, p)
        for h in range(2):
            lanes = slice(h * HALF, h * HALF + HALF)
            lr, lc, off_r, off_c = [plane[8 * h : 8 * h + 8] for plane in planes]
            sent[2 * p : 2 * p + 2, lanes] = half_targets(
                h, mine[lanes, :], inner[z, s + 2, h], strips[d][h], (corners[h], 8 * d),
                lr.astype(I32), lc.astype(I32), off_r, off_c,
            )
    sent[6:8, :] = start[0]
    sent[8:10, :] = start[1]
    sent[10:16, :] = jnp.zeros((6, VT), F32)


def own_targets(
    patches, cand, offs, pairs, start, xb, xa, rb, ra, cb, ca, lower, inner, sent,
    p0, p1, u1, t0, t1, c0, c1, cross, low,
    left, right, above, below, top, bottom, tall,
):
    row, col = tile_place()
    stack = lax.axis_index("stack").astype(I32)
    ends = slice(256, X_ROWS)
    sort_halos(col, left.at[ends], right.at[ends], xa.at[ends], xb.at[ends])
    sort_halos(row, above, below, ra, rb)
    sort_halos(row, top, bottom, ca, cb)

    def one(s, z, store, corner_first):
        d = s + z + 1

        for h in range(2):
            strip, src = (above, top) if h == 0 else (below, bottom)
            at = slice(d // 2 * 16, d // 2 * 16 + 16)
            lanes = slice(h * HALF, h * HALF + HALF)
            lr, lc = local_place(cand[s, z, :, lanes], row, col)
            store[s, :, lanes] = half_targets(
                h, patches[s, lanes, :], inner[z, s, h], strip[d], (src[at, :], corner_first), lr, lc,
                offs[s, z, 0, :, lanes].astype(F32), offs[s, z, 1, :, lanes].astype(F32),
            )

    for s in range(SEC - 1):
        one(s, 0, p0, 8 * ((s + 1) % 2))
        if s < SEC - 2:
            one(s, 1, p1, 8 * (s % 2))

    nothing = jnp.zeros((2, VT), F32)
    p0[7] = nothing
    p1[6] = nothing
    p1[7] = nothing

    tied = jnp.where(stack == 0, 0.0, lower[704:720, :].astype(F32))
    last = stack == lax.axis_size("stack") - 1
    for z, p, t, c in ((0, p0, t0, c0), (1, p1, t1, c1)):
        rows_of(p, t, 4)
        t[0:4, :] = jnp.zeros((4, VT), F32)
        c[0:4, :] = jnp.zeros((4, VT), F32)
        for s in range(SEC):
            here = jnp.full((2, VT), pairs[z, s], I32).astype(F32)
            if (s, z) in CROSS:
                n = CROSS.index((s, z))
                cross[2 * n : 2 * n + 2, :] = jnp.where(last, 0.0, here)
                here = nothing
            c[4 + 2 * s : 6 + 2 * s, :] = here
    cross[6:8, :] = nothing
    for p, (s, z) in enumerate(CROSS):
        t, c = ((t0, c0), (t1, c1))[z]
        at = 2 * (s - 6)
        t[at : at + 2, :] = sent[2 * p : 2 * p + 2, :]
        line = tied[p : p + 1, :]
        c[at : at + 2, :] = jnp.broadcast_to(jnp.concatenate([line, line], axis=1), (2, VT))
    ends = lower[720:736, :].astype(F32)
    tall[0:4, 0:HALF] = ends[0:4] + ends[8:12]
    tall[0:4, HALF:VT] = ends[4:8] + ends[12:16]
    rows_of(start, tall, 4)
    tall[20:24, :] = jnp.zeros((4, VT), F32)
    u = tall[4:20, :]

    def whole(ref):
        part = [ref[256 + 16 * n : 272 + 16 * n, :].astype(F32) for n in range(4)]
        return jnp.concatenate([part[0] + part[2], part[1] + part[3]], axis=1)

    def half(ref):
        part = ref[64:80, :].astype(F32) + ref[80:96, :].astype(F32)
        return jnp.concatenate([part, part], axis=1)

    plane = laplace(u, whole(left), whole(right), half(top), half(bottom), row, col)
    u1[...] = relaxed(u, tall, t0, t1, c0, c1, plane)
    base, own = tall[0:4, :], tall[4:8, :]
    near = jnp.concatenate([own[0:2], own[0:2]], axis=0)
    far = jnp.concatenate([jnp.zeros((2, VT), F32), own[2:4]], axis=0)
    got0 = jnp.concatenate([sent[0:2, :], sent[2:4, :]], axis=0)
    got1 = jnp.concatenate([nothing, sent[4:6, :]], axis=0)
    tied0 = jnp.concatenate([c1[0:2, :], c0[2:4, :]], axis=0)
    tied1 = jnp.concatenate([nothing, c1[2:4, :]], axis=0)
    low[0:4, :] = STEP * (tied0 * (near - base - got0) + tied1 * (far - base - got1))
    low[4:8, :] = jnp.zeros((4, VT), F32)


def sort_halos(index, first, second, p, q):
    @pl.when(index % 2 == 0)
    def _():
        first[...] = q[...]
        second[...] = p[...]

    @pl.when(index % 2 == 1)
    def _():
        first[...] = p[...]
        second[...] = q[...]


def laplace(u, left, right, above, below, row, col):
    lane = iota(u.shape, 1)
    b = lane & 15
    up = jnp.where(lane < SIDE, pltpu.roll(above, SIDE, 1), pltpu.roll(u, SIDE, 1))
    up = jnp.where((lane < SIDE) & (row == 0), u, up)
    down = jnp.where(lane >= VT - SIDE, pltpu.roll(below, VT - SIDE, 1), pltpu.roll(u, VT - SIDE, 1))
    down = jnp.where((lane >= VT - SIDE) & (row == COLS - 1), u, down)
    west = jnp.where(b == 0, pltpu.roll(left, VT - SIDE + 1, 1), pltpu.roll(u, 1, 1))
    west = jnp.where((b == 0) & (col == 0), u, west)
    east = jnp.where(b == SIDE - 1, pltpu.roll(right, SIDE - 1, 1), pltpu.roll(u, VT - 1, 1))
    east = jnp.where((b == SIDE - 1) & (col == COLS - 1), u, east)
    return ((down - u) - (u - up)) + ((east - u) - (u - west))


def relaxed(u, tall, t0, t1, c0, c1, plane):
    base = tall[0:20, :]
    s0 = c0[0:20, :] * (tall[2:22, :] - base - t0[0:20, :])
    s1 = c1[0:20, :] * (tall[4:24, :] - base - t1[0:20, :])
    zforce = s0[4:20] - s0[2:18] + s1[4:20] - s1[0:16]
    return u + STEP * (plane + zforce)


def cross_force(u, upper, got, cross):
    near, far = upper[0:2], upper[2:4]
    six = cross[0:2, :] * (near - u[12:14] - got[0:2, :])
    seven = cross[2:4, :] * (near - u[14:16] - got[2:4, :]) + cross[4:6, :] * (far - u[14:16] - got[4:6, :])
    return jnp.concatenate([jnp.zeros((12, VT), F32), six, seven], axis=0)


def first_round(start, part, got, cross, u1):
    u0 = jnp.concatenate([jnp.zeros((12, VT), F32), start[6], start[7]], axis=0)
    u1[...] = part[...] + STEP * cross_force(u0, got[6:10, :], got, cross)


def all_targets(p0, p1, got, targets):
    stack = lax.axis_index("stack").astype(I32)
    last = stack == lax.axis_size("stack") - 1
    for s in range(SEC):
        for z, p in ((0, p0), (1, p1)):
            if (s, z) in CROSS:
                n = CROSS.index((s, z))
                targets[s, z] = jnp.where(last, 0.0, got[2 * n : 2 * n + 2, :])
            else:
                targets[s, z] = p[s]


def second_round(u1, sb, sa, xa, xb, ra, rb, t0, t1, c0, c1, cross, low, got, out, tall):
    row, col = tile_place()
    stack = lax.axis_index("stack").astype(I32)
    col_even, row_even, stack_even = col % 2 == 0, row % 2 == 0, stack % 2 == 0
    u = u1[...]
    tall[4:20, :] = u
    below_rows = jnp.where(stack_even, sb[12:16, :], sa[12:16, :])
    upper = jnp.where(stack_even, sa[0:4, :], sb[0:4, :])
    tall[0:4, :] = below_rows + low[0:4, :]
    tall[20:24, :] = jnp.zeros((4, VT), F32)
    plane = laplace(
        u,
        jnp.where(col_even, xb[...], xa[...]),
        jnp.where(col_even, xa[...], xb[...]),
        jnp.where(row_even, rb[...], ra[...]),
        jnp.where(row_even, ra[...], rb[...]),
        row,
        col,
    )
    u = relaxed(u, tall, t0, t1, c0, c1, plane + cross_force(u, upper, got, cross))
    for s in range(SEC):
        out[s] = u[2 * s : 2 * s + 2]


def shape(*dims, dtype=F32):
    return jax.ShapeDtypeStruct(dims, dtype)


def call(body, outs, scratch, flops, n_in, smem=(), far=(), vmem=24 << 20):
    def space(n):
        return pltpu.SMEM if n in smem else pltpu.HBM if n in far else pltpu.VMEM

    return pl.pallas_call(
        body,
        out_shape=outs,
        in_specs=[pl.BlockSpec(memory_space=space(n)) for n in range(n_in)],
        out_specs=[pl.BlockSpec(memory_space=pltpu.VMEM) for _ in outs],
        scratch_shapes=scratch,
        name=body.__name__,
        compiler_params=pltpu.CompilerParams(vmem_limit_bytes=vmem),
        cost_estimate=pl.CostEstimate(flops=flops, bytes_accessed=1 << 20, transcendentals=0),
    )


def on_device(patches, cand, offs, pairs, start):
    pairs = pairs.T
    flat = pltpu.VMEM((16, VT), F32)
    held = [
        pltpu.VMEM((SEC, VT, PATCH), BF),
        pltpu.VMEM((2, 2, 8, VT), I32),
        pltpu.VMEM((2, 2, 2, 8, VT), I32),
        pltpu.VMEM((2, SEC), I32),
        pltpu.VMEM((SEC, 2, VT), F32),
        pltpu.SemaphoreType.DMA((4 + SEC,)),
    ]
    outs = [shape(SEC, 32, PATCH, dtype=BF)] * 2 + [shape(X_ROWS, PATCH, dtype=BF)] * 2 + [shape(S_ROWS, PATCH, dtype=BF)]
    outs = [pltpu.VMEM(a.shape, a.dtype) for a in outs]
    rb, ra, xb, xa, lower = call(pack_first, outs, [flat] + held, 1 << 20, 5, far=(0, 1, 2, 3, 4), vmem=58 << 20)(
        patches, cand, offs, pairs, start
    )
    rb = swapped(rb, "tile", row_b)
    ra = swapped(ra, "tile", row_a)
    xa = swapped(xa, "tile", col_a)
    xb = swapped(xb, "tile", col_b)
    lower = swapped(lower, "stack", lambda i: (i + 1) % 16)
    cb, ca = call(pack_corners, [shape(C_ROWS, PATCH, dtype=BF)] * 2, [flat], 1 << 20, 3)(start, xb, xa)
    cb = swapped(cb, "tile", row_b)
    ca = swapped(ca, "tile", row_a)
    halos = (xb, xa, rb, ra, cb, ca)
    (inner,) = call(
        inner_scores, [shape(2, SEC + 2, 2, 8, HALF)], [pltpu.VMEM((X_ROWS, PATCH), BF)] * 2, 1 << 31, 5
    )(patches, cand, xb, xa, lower)
    (sent,) = call(lower_targets, [shape(16, VT)], [], 1 << 20, 7)(start, rb, ra, cb, ca, lower, inner)
    got = swapped(sent, "stack", lambda i: (i - 1) % 16)
    p0, p1, part, t0, t1, c0, c1, cross, low = call(
        own_targets,
        [shape(SEC, 2, VT)] * 2 + [shape(16, VT)] + [shape(24, VT)] * 4 + [shape(8, VT)] * 2,
        [pltpu.VMEM(a.shape, BF) for a in halos] + [pltpu.VMEM((24, VT), F32)],
        1 << 31,
        14,
        smem=(3,),
    )(patches, cand, offs, pairs, start, *halos, lower, inner, sent)
    sa = swapped(part, "stack", stack_a)
    sb = swapped(part, "stack", stack_b)
    (u1,) = call(first_round, [shape(16, VT)], [], 1 << 16, 4)(start, part, got, cross)
    moved = [swapped(u1, "tile", partner) for partner in (col_a, col_b, row_a, row_b)]
    (targets,) = call(all_targets, [shape(SEC, 2, 2, VT)], [], 1 << 20, 3)(p0, p1, got)
    (aligned,) = call(second_round, [shape(SEC, 2, VT)], [pltpu.VMEM((24, VT), F32)], 1 << 20, 14)(
        u1, sb, sa, *moved, t0, t1, c0, c1, cross, low, got
    )
    return aligned, targets


def solution(mesh):
    placed = (
        P("stack", "tile", None),
        P("stack", None, None, "tile"),
        P("stack", None, None, None, "tile"),
        P("stack", None),
        P("stack", None, "tile"),
    )
    return jax.shard_map(
        on_device,
        mesh=mesh,
        in_specs=placed,
        out_specs=(P("stack", None, "tile"), P("stack", None, None, "tile")),
        check_vma=False,
    )
```
